128 devices in a mesh: ctx: 64 (over z, x, y_hi, core), grp: 2 (over y_lo).
Axes of the slice: x: 4, y: 4 (y_hi: 2, y_lo: 2; y = y_hi * 2 + y_lo), z: 4, core: 2. Of those that a mesh axis runs over, the one named last changes fastest.
Arguments:
- queries: bfloat16 [16384, 1024], P('ctx', 'grp'), parts along dimension 1, may hold values from -5.5 to 5.5
- key_rows: bfloat16 [16384, 256], P('ctx', 'grp'), parts along dimension 1, may hold values from -5.5 to 5.5
- value_rows: bfloat16 [16384, 256], P('ctx', 'grp'), parts along dimension 1, may hold values from -6 to 6
Outputs:
- attended: bfloat16 [16384, 1024], P('ctx', 'grp'), parts along dimension 1
The draws below stay inside these ranges and needn't reach their ends.
There are 2 independent parts, one for each index of `grp`. The reference program is written for one: setup_inputs(seed, part) draws one part's arguments, and reference() takes and returns one part's arrays. A program takes and returns all parts, laid end to end along the dimension named above; each array names one. Nothing has to cross between parts.
All inputs are finite; a program needn't handle non-finite values.
Results may differ from the reference program's by a relative error of at most 0.0029.
Values may be sent and summed in bfloat16 or wider, within the bound.
A program may use at most 192 MiB of HBM per device.

```python
import jax
import jax.numpy as jnp
from jax import lax

HEADS = 4
HD = 128
TOKENS = 16384


def draw_queries(key, part):
    key = jax.random.fold_in(key, 11)
    base_key, scale_key = jax.random.split(key)
    row_total = TOKENS
    lane_total = HEADS * HD
    row_scale = jnp.exp(jax.random.uniform(scale_key, (row_total, 1), jnp.float32, jnp.log(0.7), jnp.log(1.7)))
    base_values = jnp.clip(1.6 * jax.random.normal(base_key, (row_total, lane_total), jnp.float32), -3.2, 3.2)
    result = base_values * row_scale
    return result.astype(jnp.bfloat16)


def draw_key_rows(key, part):
    key = jax.random.fold_in(key, 23)
    base_key, scale_key = jax.random.split(key)
    row_total = TOKENS
    row_scale = jnp.exp(jax.random.uniform(scale_key, (row_total, 1), jnp.float32, jnp.log(0.7), jnp.log(1.7)))
    base_values = jnp.clip(1.6 * jax.random.normal(base_key, (row_total, HD), jnp.float32), -3.2, 3.2)
    result = base_values * row_scale
    return result.astype(jnp.bfloat16)


def levels(rng, shape, pieces, smallest, high):
    def one(dim, parts):
        draws = jax.random.uniform(jax.random.fold_in(jax.random.fold_in(rng, 6), dim), (parts,), jnp.float32, smallest / len(pieces), high / len(pieces))
        return jnp.repeat(jnp.exp(draws), shape[dim] // parts).reshape((-1,) + (1,) * (len(shape) - dim - 1))

    level = one(*pieces[0])
    for cut in pieces[1:]:
        level = level * one(*cut)
    return level


def centred(own_key, extent, deviation, most, shards=(), kind=jnp.bfloat16):
    loudness = levels(own_key, extent, shards, -0.22, 0.18) if shards else 1.0
    drawn = jax.random.normal(own_key, extent, jnp.float32) * deviation * loudness
    return jnp.minimum(jnp.maximum(drawn, -most), most).astype(kind)


def setup_inputs(seed: int = 0, part: int = 0) -> dict:
    key_list = jax.random.split(jax.random.key(seed), 4)
    own_keys = jax.random.split(jax.random.fold_in(key_list[3], part), 4)
    queries = draw_queries(jax.random.fold_in(jax.random.fold_in(key_list[3], part), 71), part)
    key_rows = draw_key_rows(jax.random.fold_in(jax.random.fold_in(key_list[3], part), 71), part)
    value_rows = centred(own_keys[2], (TOKENS, HD), 1.0, 6.0, ((0, 64),))
    return {"queries": queries, "key_rows": key_rows, "value_rows": value_rows}


masked_fill = -1e30


def reference(queries, key_rows, value_rows):
    block_size = 256
    block_count = TOKENS // block_size
    score_scale = 1.0 / (HD ** 0.5)
    key_float = key_rows.astype(jnp.float32)
    value_float = value_rows.astype(jnp.float32)
    key_pos = jnp.arange(TOKENS, dtype=jnp.int32)
    query_blocks = queries.reshape(block_count, block_size, HEADS, HD)
    first_rows = (jnp.arange(block_count, dtype=jnp.int32) * block_size).astype(jnp.int32)

    def block_attend(inputs):
        query_block, first_row = inputs
        scores = jnp.einsum('qhd,kd->qhk', query_block.astype(jnp.float32), key_float) * score_scale
        query_pos = first_row + jnp.arange(block_size, dtype=jnp.int32)
        visible = key_pos[None, None, :] <= query_pos[:, None, None]
        scores = jnp.where(visible, scores, masked_fill)
        row_max = jnp.max(scores, axis=-1)
        weights = jnp.where(visible, jnp.exp(scores - row_max[..., None]), jnp.float32(0.0))
        total = jnp.sum(weights, axis=-1)
        rounded = lax.optimization_barrier(weights.astype(jnp.bfloat16))
        summed = jnp.einsum('qhk,kd->qhd', rounded.astype(jnp.float32), value_float)
        return (summed / total[..., None]).astype(jnp.bfloat16).reshape(block_size, HEADS * HD)

    attended = lax.map(block_attend, (query_blocks, first_rows))
    return attended.reshape(TOKENS, HEADS * HD)
```

```python
import math

import jax
import jax.numpy as jnp
from jax import lax
from jax.experimental import pallas as pl
from jax.experimental.pallas import tpu as pltpu
from jax.sharding import PartitionSpec as P

MESH = pl.DeviceIdType.MESH
F32 = jnp.float32
BF16 = jnp.bfloat16
LOW = -1e30
ROWS = 256
HD = 128
HEADS = 4
COLS = ROWS * HEADS
PLACES = 16
EARLY = 3


def dot(a, b):
    return lax.dot_general(a, b, (((1,), (0,)), ((), ())), preferred_element_type=F32)


def kernel(
    q_ref, k_ref, v_ref, out_ref,
    blocks, q_other, q_t, m_ref, l_ref, acc, s_a, s_b, p_a, p_b, al_a, al_b,
    part_o, part_ml, got_o, got_ml,
    to_sem, from_sem, pass_sem, passed_sem, q_sems, part_sems, ml_sems,
):
    ctx = lax.axis_index("ctx")
    grp = lax.axis_index("grp")
    place = ctx // 4
    y = (ctx // 2) % 2
    core = ctx % 2
    sibling = (ctx + 1 - 2 * core, grp)
    partner = (ctx + 2 - 4 * y, grp)
    pairs = place // 2
    odd = place % 2

    def at(other_place):
        return (other_place * 4 + y * 2 + core, grp)

    barrier = pltpu.get_barrier_semaphore()
    pl.semaphore_signal(barrier, inc=1, device_id=sibling, device_id_type=MESH)
    pl.semaphore_signal(barrier, inc=1, device_id=partner, device_id_type=MESH)

    def greet(i, _):
        pl.semaphore_signal(barrier, inc=1, device_id=at(i), device_id_type=MESH)
        return 0

    lax.fori_loop(0, place, greet, 0)

    mine = place * 2 + core
    blocks[mine, :ROWS] = k_ref[...]
    v_t = jnp.transpose(v_ref[...].astype(F32)).astype(BF16)
    blocks[mine, ROWS : ROWS + HD] = v_t[:, :HD]
    blocks[mine, ROWS + HD :] = v_t[:, HD:]

    pl.semaphore_wait(barrier, 17 - place)

    def copy(src, dst, send, recv, device):
        return pltpu.make_async_remote_copy(
            src_ref=src, dst_ref=dst, send_sem=send, recv_sem=recv,
            device_id=device, device_id_type=MESH,
        )

    def block_to(other_place):
        return copy(
            blocks.at[mine], blocks.at[mine], to_sem.at[other_place], from_sem.at[place], at(other_place)
        )

    def block_from(other_place):
        here = other_place * 2 + core
        return copy(
            blocks.at[here], blocks.at[here], to_sem.at[other_place], from_sem.at[other_place], at(other_place)
        )

    def block_pass(other_place):
        here = other_place * 2 + core
        return copy(
            blocks.at[here], blocks.at[here], pass_sem.at[other_place], passed_sem.at[other_place], sibling
        )

    def block_passed(other_place):
        here = other_place * 2 + 1 - core
        return copy(
            blocks.at[here], blocks.at[here], pass_sem.at[other_place], passed_sem.at[other_place], sibling
        )

    q_copy = copy(q_ref, q_other, q_sems.at[0], q_sems.at[1], partner)
    block_pass(place).start()
    q_copy.start()

    def send(i, _):
        block_to(i).start()
        return 0

    lax.fori_loop(place + 1, PLACES, send, 0)

    scale = math.log2(math.e) / math.sqrt(HD)

    def ready_queries(ref, s):
        for h in range(HEADS):
            full = jnp.transpose(ref[:, h * HD : (h + 1) * HD].astype(F32)) * scale
            hi = full.astype(BF16)
            q_t[s, :HD, h * ROWS : (h + 1) * ROWS] = hi
            q_t[s, HD:, h * ROWS : (h + 1) * ROWS] = (full - hi.astype(F32)).astype(BF16)

    m_ref[...] = jnp.full(m_ref.shape, LOW, F32)
    l_ref[...] = jnp.zeros(l_ref.shape, F32)
    acc[...] = jnp.zeros(acc.shape, F32)
    ready_queries(q_ref, 0)

    s_refs, p_refs, al_refs = (s_a, s_b), (p_a, p_b), (al_a, al_b)

    def keys(first, count):
        k = jnp.concatenate([blocks[first + i, :ROWS] for i in range(count)], 0)
        return jnp.concatenate([k, k], 1)

    def values(first, count):
        tiles = []
        for i in range(count):
            tiles.append(blocks[first + i, ROWS : ROWS + HD])
            tiles.append(blocks[first + i, ROWS + HD :])
        return jnp.concatenate(tiles, 1)

    def cols(h):
        return slice(h * ROWS, (h + 1) * ROWS)

    def scores(s, k, h, slot):
        s_refs[slot][: k.shape[0]] = dot(k, q_t[s, :, cols(h)])

    def weigh(s, h, slot, count, masked):
        n = count * ROWS
        score = s_refs[slot][:n]
        if masked:
            key_at = lax.broadcasted_iota(jnp.int32, (n, ROWS), 0)
            query_at = lax.broadcasted_iota(jnp.int32, (n, ROWS), 1) + core * ROWS
            score = jnp.where(key_at <= query_at, score, LOW)
        old = m_ref[s, :, cols(h)]
        top = jnp.max(score.reshape(n // 8, 8, ROWS), axis=0)
        new = jnp.maximum(old, jnp.max(top, axis=0, keepdims=True))
        w = jnp.exp2(score - new[:1])
        alpha = jnp.exp2(old - new)
        l_ref[s, :, cols(h)] = l_ref[s, :, cols(h)] * alpha + jnp.sum(w.reshape(n // 8, 8, ROWS), axis=0)
        p_refs[slot][:n] = w.astype(BF16)
        al_refs[slot][...] = alpha
        m_ref[s, :, cols(h)] = new

    def gather(s, v, h, slot):
        n = v.shape[1]
        acc[s, :, cols(h)] = acc[s, :, cols(h)] * al_refs[slot][:1] + dot(v, p_refs[slot][:n])

    def one_place(s, other_place, masked):
        first = other_place * 2
        k, v = keys(first, 2), values(first, 2)
        scores(s, k, 0, 0)
        for h in range(HEADS):
            if h + 1 < HEADS:
                scores(s, k, h + 1, (h + 1) % 2)
            if h > 0:
                gather(s, v, h - 1, (h - 1) % 2)
            weigh(s, h, h % 2, 2, masked)
        gather(s, v, HEADS - 1, (HEADS - 1) % 2)

    def first_block(t):
        return 4 * (pairs - 1 - t)

    def arrive(t):
        @pl.when(t < pairs)
        def _():
            for other_place in (2 * (pairs - 1 - t) + 1, 2 * (pairs - 1 - t)):
                block_from(other_place).wait_recv()
                block_pass(other_place).start()

    def complete(t):
        @pl.when(t < pairs)
        def _():
            for other_place in (2 * (pairs - 1 - t) + 1, 2 * (pairs - 1 - t)):
                block_passed(other_place).wait_recv()

    def phase(s, lo, hi, wait_from):
        @pl.when(lo < hi)
        def _():
            scores(s, keys(first_block(lo), 4), 0, 0)
            p_b[...] = jnp.zeros(p_b.shape, BF16)
            al_b[...] = jnp.ones(al_b.shape, F32)

            def item(t, _):
                if wait_from is not None:
                    @pl.when(t >= wait_from)
                    def _():
                        arrive(t + 2)
                        complete(t + 1)
                k, v = keys(first_block(t), 4), values(first_block(t), 4)
                k_next = keys(first_block(jnp.minimum(t + 1, hi - 1)), 4)
                v_last = values(first_block(jnp.maximum(t - 1, lo)), 4)
                for h in range(HEADS):
                    if h + 1 < HEADS:
                        scores(s, k, h + 1, (h + 1) % 2)
                    else:
                        scores(s, k_next, 0, 0)
                    if h > 0:
                        gather(s, v, h - 1, (h - 1) % 2)
                    else:
                        gather(s, v_last, HEADS - 1, 1)
                    weigh(s, h, h % 2, 4, False)
                return 0

            lax.fori_loop(lo, hi, item, 0)
            gather(s, values(first_block(hi - 1), 4), HEADS - 1, 1)

    block_passed(place).wait_recv()
    one_place(0, place, True)

    @pl.when(odd == 1)
    def _():
        block_from(place - 1).wait_recv()
        block_pass(place - 1).start()

    arrive(0)

    @pl.when(odd == 1)
    def _():
        block_passed(place - 1).wait_recv()
        one_place(0, place - 1, False)

    arrive(1)
    complete(0)
    early = jnp.minimum(pairs, EARLY)
    phase(0, 0, early, 0)

    q_copy.wait_recv()
    ready_queries(q_other, 1)

    @pl.when(y == 0)
    def _():
        one_place(1, place, False)

    @pl.when(odd == 1)
    def _():
        one_place(1, place - 1, False)

    phase(1, 0, pairs, EARLY)
    l_other = jnp.sum(l_ref[1], axis=0, keepdims=True)
    part_o[...] = (acc[1] / jnp.where(l_other > 0, l_other, 1.0)).astype(BF16)
    part_ml[0:1] = m_ref[1, 0:1]
    part_ml[1:2] = l_other
    part_ml[2:] = jnp.zeros((6, COLS), F32)
    o_copy = copy(part_o, got_o, part_sems.at[0], part_sems.at[1], partner)
    ml_copy = copy(part_ml, got_ml, ml_sems.at[0], ml_sems.at[1], partner)
    o_copy.start()
    ml_copy.start()

    phase(0, early, pairs, None)

    o_copy.wait_recv()
    ml_copy.wait_recv()
    m_own, m_got = m_ref[0, 0:1], got_ml[0:1]
    top = jnp.maximum(m_own, m_got)
    a_own = jnp.exp2(m_own - top)
    a_got = jnp.exp2(m_got - top) * got_ml[1:2]
    total = jnp.sum(l_ref[0], axis=0, keepdims=True) * a_own + a_got
    f_own, f_got = a_own / total, a_got / total
    for h in range(HEADS):
        o = acc[0, :, cols(h)] * f_own[:, cols(h)] + got_o[:, cols(h)].astype(F32) * f_got[:, cols(h)]
        out_ref[:, h * HD : (h + 1) * HD] = jnp.transpose(o).astype(BF16)

    o_copy.wait_send()
    ml_copy.wait_send()
    q_copy.wait_send()

    def sent(i, _):
        block_to(i).wait_send()
        return 0

    lax.fori_loop(place + 1, PLACES, sent, 0)

    def passed_on(i, _):
        block_pass(i).wait_send()
        return 0

    lax.fori_loop(0, place + 1, passed_on, 0)


def per_device(queries, key_rows, value_rows):
    vmem = pl.BlockSpec(memory_space=pltpu.VMEM)
    return pl.pallas_call(
        kernel,
        out_shape=jax.ShapeDtypeStruct((ROWS, HEADS * HD), BF16),
        in_specs=[vmem] * 3,
        out_specs=vmem,
        scratch_shapes=[
            pltpu.VMEM((PLACES * 2, 2 * ROWS, HD), BF16),
            pltpu.VMEM((ROWS, HEADS * HD), BF16),
            pltpu.VMEM((2, 2 * HD, COLS), BF16),
            pltpu.VMEM((2, 8, COLS), F32),
            pltpu.VMEM((2, 8, COLS), F32),
            pltpu.VMEM((2, HD, COLS), F32),
            pltpu.VMEM((4 * ROWS, ROWS), F32),
            pltpu.VMEM((4 * ROWS, ROWS), F32),
            pltpu.VMEM((4 * ROWS, ROWS), BF16),
            pltpu.VMEM((4 * ROWS, ROWS), BF16),
            pltpu.VMEM((8, ROWS), F32),
            pltpu.VMEM((8, ROWS), F32),
            pltpu.VMEM((HD, COLS), BF16),
            pltpu.VMEM((8, COLS), F32),
            pltpu.VMEM((HD, COLS), BF16),
            pltpu.VMEM((8, COLS), F32),
            pltpu.SemaphoreType.DMA((PLACES,)),
            pltpu.SemaphoreType.DMA((PLACES,)),
            pltpu.SemaphoreType.DMA((PLACES,)),
            pltpu.SemaphoreType.DMA((PLACES,)),
            pltpu.SemaphoreType.DMA((2,)),
            pltpu.SemaphoreType.DMA((2,)),
            pltpu.SemaphoreType.DMA((2,)),
        ],
        compiler_params=pltpu.CompilerParams(
            collective_id=0, has_side_effects=True, vmem_limit_bytes=48 << 20
        ),
        name="attend",
    )(queries, key_rows, value_rows)


def solution(mesh):
    placed = (P("ctx", "grp"), P("ctx", "grp"), P("ctx", "grp"))
    return jax.shard_map(
        per_device, mesh=mesh, in_specs=placed, out_specs=P("ctx", "grp"), check_vma=False
    )
```

```python
import math

import jax
import jax.numpy as jnp
from jax import lax
from jax.experimental import pallas as pl
from jax.experimental.pallas import tpu as pltpu
from jax.sharding import PartitionSpec as P

MESH = pl.DeviceIdType.MESH
F32 = jnp.float32
BF16 = jnp.bfloat16
LOW = -1e30
ROWS = 256
HD = 128
HEADS = 4
COLS = ROWS * HEADS
PLACES = 16
EARLY = 3


def dot(a, b):
    return lax.dot_general(a, b, (((1,), (0,)), ((), ())), preferred_element_type=F32)


def kernel(
    q_ref, k_ref, v_ref, out_ref,
    blocks, q_other, q_t, m_ref, l_ref, acc, s_a, s_b, p_a, p_b, al_a, al_b,
    part_o, part_ml, got_o, got_ml,
    x_sem, z_sem, from_sem, pass_sem, passed_sem, q_sems, part_sems, ml_sems,
):
    ctx = lax.axis_index("ctx")
    grp = lax.axis_index("grp")
    place = ctx // 4
    y = (ctx // 2) % 2
    core = ctx % 2
    sibling = (ctx + 1 - 2 * core, grp)
    partner = (ctx + 2 - 4 * y, grp)
    pairs = place // 2
    odd = place % 2
    z, x = place // 4, place % 4
    along_x = core == 0

    def at(other_place):
        return (other_place * 4 + y * 2 + core, grp)

    def mates(step):
        for dx in (1, 3, 2):
            mate = (x + dx) % 4
            through = jnp.logical_or(jnp.logical_and(along_x, z < 3), jnp.logical_and(core == 1, z > 0))
            step(mate, jnp.logical_or(through, mate > x), jnp.logical_or(through, mate < x))

    barrier = pltpu.get_barrier_semaphore()
    pl.semaphore_signal(barrier, inc=1, device_id=sibling, device_id_type=MESH)
    pl.semaphore_signal(barrier, inc=1, device_id=partner, device_id_type=MESH)

    def greet(mate, _, hears):
        @pl.when(hears)
        def _():
            pl.semaphore_signal(barrier, inc=1, device_id=at(z * 4 + mate), device_id_type=MESH)

    mates(greet)
    for below in range(3):
        @pl.when(below < z)
        def _(below=below):
            pl.semaphore_signal(barrier, inc=1, device_id=at(below * 4 + x), device_id_type=MESH)

    mine = place * 2 + core
    blocks[mine, :ROWS] = k_ref[...]
    v_t = jnp.transpose(v_ref[...].astype(F32)).astype(BF16)
    blocks[mine, ROWS : ROWS + HD] = v_t[:, :HD]
    blocks[mine, ROWS + HD :] = v_t[:, HD:]

    through = jnp.where(along_x, z < 3, z > 0)
    pl.semaphore_wait(barrier, 5 - z + jnp.where(through, 3, 3 - x))

    def copy(src, dst, send, recv, device):
        return pltpu.make_async_remote_copy(
            src_ref=src, dst_ref=dst, send_sem=send, recv_sem=recv,
            device_id=device, device_id_type=MESH,
        )

    def along_x_copy(plane, mate):
        here = (plane * 4 + x) * 2 + core
        return copy(
            blocks.at[here], blocks.at[here], x_sem.at[plane, mate], from_sem.at[plane * 4 + x], at(z * 4 + mate)
        )

    def along_z_copy(column, above):
        here = (z * 4 + column) * 2 + core
        return copy(
            blocks.at[here], blocks.at[here], z_sem.at[column, above], from_sem.at[z * 4 + column], at(above * 4 + x)
        )

    def up(column, step):
        for dz in (1, 2, 3):
            @pl.when(z + dz < 4)
            def _(dz=dz):
                step(along_z_copy(column, z + dz))

    def across(plane, step):
        for dx in (1, 3, 2):
            step(along_x_copy(plane, (x + dx) % 4))

    def own_across(step):
        def one(mate, sends, _):
            @pl.when(jnp.logical_or(jnp.logical_and(along_x, z < 3), mate > x))
            def _():
                step(along_x_copy(z, mate))

        mates(one)

    def block_from(other_place):
        here = other_place * 2 + core
        return copy(
            blocks.at[here], blocks.at[here], x_sem.at[0, 0], from_sem.at[other_place], sibling
        )

    def block_pass(other_place):
        here = other_place * 2 + core
        return copy(
            blocks.at[here], blocks.at[here], pass_sem.at[other_place], passed_sem.at[other_place], sibling
        )

    def block_passed(other_place):
        here = other_place * 2 + 1 - core
        return copy(
            blocks.at[here], blocks.at[here], pass_sem.at[other_place], passed_sem.at[other_place], sibling
        )

    q_copy = copy(q_ref, q_other, q_sems.at[0], q_sems.at[1], partner)
    block_pass(place).start()
    q_copy.start()

    def start(c):
        c.start()

    @pl.when(core == 0)
    def _():
        own_across(start)
        up(x, start)

    @pl.when(core == 1)
    def _():
        up(x, start)
        own_across(start)

    scale = math.log2(math.e) / math.sqrt(HD)

    def ready_queries(ref, s):
        for h in range(HEADS):
            full = jnp.transpose(ref[:, h * HD : (h + 1) * HD].astype(F32)) * scale
            hi = full.astype(BF16)
            q_t[s, :HD, h * ROWS : (h + 1) * ROWS] = hi
            q_t[s, HD:, h * ROWS : (h + 1) * ROWS] = (full - hi.astype(F32)).astype(BF16)

    m_ref[...] = jnp.full(m_ref.shape, LOW, F32)
    l_ref[...] = jnp.zeros(l_ref.shape, F32)
    acc[...] = jnp.zeros(acc.shape, F32)
    ready_queries(q_ref, 0)

    s_refs, p_refs, al_refs = (s_a, s_b), (p_a, p_b), (al_a, al_b)

    def keys(first, count):
        k = jnp.concatenate([blocks[first + i, :ROWS] for i in range(count)], 0)
        return jnp.concatenate([k, k], 1)

    def values(first, count):
        tiles = []
        for i in range(count):
            tiles.append(blocks[first + i, ROWS : ROWS + HD])
            tiles.append(blocks[first + i, ROWS + HD :])
        return jnp.concatenate(tiles, 1)

    def cols(h):
        return slice(h * ROWS, (h + 1) * ROWS)

    def scores(s, k, h, slot):
        s_refs[slot][: k.shape[0]] = dot(k, q_t[s, :, cols(h)])

    def weigh(s, h, slot, count, masked):
        n = count * ROWS
        score = s_refs[slot][:n]
        if masked:
            key_at = lax.broadcasted_iota(jnp.int32, (n, ROWS), 0)
            query_at = lax.broadcasted_iota(jnp.int32, (n, ROWS), 1) + core * ROWS
            score = jnp.where(key_at <= query_at, score, LOW)
        old = m_ref[s, :, cols(h)]
        top = jnp.max(score.reshape(n // 8, 8, ROWS), axis=0)
        new = jnp.maximum(old, jnp.max(top, axis=0, keepdims=True))
        w = jnp.exp2(score - new[:1])
        alpha = jnp.exp2(old - new)
        l_ref[s, :, cols(h)] = l_ref[s, :, cols(h)] * alpha + jnp.sum(w.reshape(n // 8, 8, ROWS), axis=0)
        p_refs[slot][:n] = w.astype(BF16)
        al_refs[slot][...] = alpha
        m_ref[s, :, cols(h)] = new

    def gather(s, v, h, slot):
        n = v.shape[1]
        acc[s, :, cols(h)] = acc[s, :, cols(h)] * al_refs[slot][:1] + dot(v, p_refs[slot][:n])

    def one_place(s, other_place, masked):
        first = other_place * 2
        k, v = keys(first, 2), values(first, 2)
        scores(s, k, 0, 0)
        for h in range(HEADS):
            if h + 1 < HEADS:
                scores(s, k, h + 1, (h + 1) % 2)
            if h > 0:
                gather(s, v, h - 1, (h - 1) % 2)
            weigh(s, h, h % 2, 2, masked)
        gather(s, v, HEADS - 1, (HEADS - 1) % 2)

    def first_block(t):
        return 4 * (pairs - 1 - t)

    def take(other_place):
        relayed = jnp.where(along_x, other_place // 4 == z, other_place % 4 == x)

        @pl.when(jnp.logical_not(relayed))
        def _():
            block_from(other_place).wait_recv()
            block_pass(other_place).start()

    def arrive(t):
        @pl.when(t < pairs)
        def _():
            take(2 * (pairs - 1 - t) + 1)
            take(2 * (pairs - 1 - t))

    def relay(step_up, step_across):
        @pl.when(core == 0)
        def _():
            def one(mate, _, hears):
                @pl.when(hears)
                def _():
                    step_up(mate)

            mates(one)

        @pl.when(core == 1)
        def _():
            for dz in (1, 2, 3):
                @pl.when(z >= dz)
                def _(dz=dz):
                    step_across(z - dz)

    def relay_up(mate):
        block_from(z * 4 + mate).wait_recv()
        up(mate, start)

        @pl.when(mate < x)
        def _():
            block_pass(z * 4 + mate).start()

    def relay_across(plane):
        block_from(plane * 4 + x).wait_recv()
        across(plane, start)
        block_pass(plane * 4 + x).start()

    def complete(t):
        @pl.when(t < pairs)
        def _():
            for other_place in (2 * (pairs - 1 - t) + 1, 2 * (pairs - 1 - t)):
                block_passed(other_place).wait_recv()

    def phase(s, lo, hi, wait_from):
        @pl.when(lo < hi)
        def _():
            scores(s, keys(first_block(lo), 4), 0, 0)
            p_b[...] = jnp.zeros(p_b.shape, BF16)
            al_b[...] = jnp.ones(al_b.shape, F32)

            def item(t, _):
                if wait_from is not None:
                    @pl.when(t >= wait_from)
                    def _():
                        arrive(t + 2)
                        complete(t + 1)
                k, v = keys(first_block(t), 4), values(first_block(t), 4)
                k_next = keys(first_block(jnp.minimum(t + 1, hi - 1)), 4)
                v_last = values(first_block(jnp.maximum(t - 1, lo)), 4)
                for h in range(HEADS):
                    if h + 1 < HEADS:
                        scores(s, k, h + 1, (h + 1) % 2)
                    else:
                        scores(s, k_next, 0, 0)
                    if h > 0:
                        gather(s, v, h - 1, (h - 1) % 2)
                    else:
                        gather(s, v_last, HEADS - 1, 1)
                    weigh(s, h, h % 2, 4, False)
                return 0

            lax.fori_loop(lo, hi, item, 0)
            gather(s, values(first_block(hi - 1), 4), HEADS - 1, 1)

    block_passed(place).wait_recv()
    one_place(0, place, True)
    relay(relay_up, relay_across)

    @pl.when(odd == 1)
    def _():
        take(place - 1)

    arrive(0)

    @pl.when(odd == 1)
    def _():
        block_passed(place - 1).wait_recv()
        one_place(0, place - 1, False)

    arrive(1)
    complete(0)
    early = jnp.minimum(pairs, EARLY)
    phase(0, 0, early, 0)

    q_copy.wait_recv()
    ready_queries(q_other, 1)

    @pl.when(y == 0)
    def _():
        one_place(1, place, False)

    @pl.when(odd == 1)
    def _():
        one_place(1, place - 1, False)

    phase(1, 0, pairs, EARLY)
    l_other = jnp.sum(l_ref[1], axis=0, keepdims=True)
    part_o[...] = (acc[1] / jnp.where(l_other > 0, l_other, 1.0)).astype(BF16)
    part_ml[0:1] = m_ref[1, 0:1]
    part_ml[1:2] = l_other
    part_ml[2:] = jnp.zeros((6, COLS), F32)
    o_copy = copy(part_o, got_o, part_sems.at[0], part_sems.at[1], partner)
    ml_copy = copy(part_ml, got_ml, ml_sems.at[0], ml_sems.at[1], partner)
    o_copy.start()
    ml_copy.start()

    phase(0, early, pairs, None)

    o_copy.wait_recv()
    ml_copy.wait_recv()
    m_own, m_got = m_ref[0, 0:1], got_ml[0:1]
    top = jnp.maximum(m_own, m_got)
    a_own = jnp.exp2(m_own - top)
    a_got = jnp.exp2(m_got - top) * got_ml[1:2]
    total = jnp.sum(l_ref[0], axis=0, keepdims=True) * a_own + a_got
    f_own, f_got = a_own / total, a_got / total
    for h in range(HEADS):
        o = acc[0, :, cols(h)] * f_own[:, cols(h)] + got_o[:, cols(h)].astype(F32) * f_got[:, cols(h)]
        out_ref[:, h * HD : (h + 1) * HD] = jnp.transpose(o).astype(BF16)

    o_copy.wait_send()
    ml_copy.wait_send()
    q_copy.wait_send()

    def gone(c):
        c.wait_send()

    own_across(gone)
    up(x, gone)
    relay(lambda mate: up(mate, gone), lambda plane: across(plane, gone))

    def passed_on(i, _):
        block_pass(i).wait_send()
        return 0

    lax.fori_loop(0, place + 1, passed_on, 0)


def per_device(queries, key_rows, value_rows):
    vmem = pl.BlockSpec(memory_space=pltpu.VMEM)
    return pl.pallas_call(
        kernel,
        out_shape=jax.ShapeDtypeStruct((ROWS, HEADS * HD), BF16),
        in_specs=[vmem] * 3,
        out_specs=vmem,
        scratch_shapes=[
            pltpu.VMEM((PLACES * 2, 2 * ROWS, HD), BF16),
            pltpu.VMEM((ROWS, HEADS * HD), BF16),
            pltpu.VMEM((2, 2 * HD, COLS), BF16),
            pltpu.VMEM((2, 8, COLS), F32),
            pltpu.VMEM((2, 8, COLS), F32),
            pltpu.VMEM((2, HD, COLS), F32),
            pltpu.VMEM((4 * ROWS, ROWS), F32),
            pltpu.VMEM((4 * ROWS, ROWS), F32),
            pltpu.VMEM((4 * ROWS, ROWS), BF16),
            pltpu.VMEM((4 * ROWS, ROWS), BF16),
            pltpu.VMEM((8, ROWS), F32),
            pltpu.VMEM((8, ROWS), F32),
            pltpu.VMEM((HD, COLS), BF16),
            pltpu.VMEM((8, COLS), F32),
            pltpu.VMEM((HD, COLS), BF16),
            pltpu.VMEM((8, COLS), F32),
            pltpu.SemaphoreType.DMA((4, 4)),
            pltpu.SemaphoreType.DMA((4, 4)),
            pltpu.SemaphoreType.DMA((PLACES,)),
            pltpu.SemaphoreType.DMA((PLACES,)),
            pltpu.SemaphoreType.DMA((PLACES,)),
            pltpu.SemaphoreType.DMA((2,)),
            pltpu.SemaphoreType.DMA((2,)),
            pltpu.SemaphoreType.DMA((2,)),
        ],
        compiler_params=pltpu.CompilerParams(
            collective_id=0, has_side_effects=True, vmem_limit_bytes=48 << 20
        ),
        name="attend",
    )(queries, key_rows, value_rows)


def solution(mesh):
    placed = (P("ctx", "grp"), P("ctx", "grp"), P("ctx", "grp"))
    return jax.shard_map(
        per_device, mesh=mesh, in_specs=placed, out_specs=P("ctx", "grp"), check_vma=False
    )
```

```python
import math

import jax
import jax.numpy as jnp
from jax import lax
from jax.experimental import pallas as pl
from jax.experimental.pallas import tpu as pltpu
from jax.sharding import PartitionSpec as P

MESH = pl.DeviceIdType.MESH
F32 = jnp.float32
BF16 = jnp.bfloat16
LOW = -1e30
ROWS = 256
HD = 128
HEADS = 4
COLS = ROWS * HEADS
PLACES = 16
KEYS = 4 * ROWS
SETS = 4


def dot(a, b):
    return lax.dot_general(a, b, (((1,), (0,)), ((), ())), preferred_element_type=F32)


def kernel(
    q_in, k_in, v_in, out_ref,
    blocks, v_own, q_sets, q_t, ml_ref, acc, s_a, s_b, p_a, p_b, al_a, al_b,
    got_acc, got_ml, part_o, part_ml, got_o, got_oml,
    in_sem, x_sem, z_sem, from_sem, q_send, q_recv, acc_send, acc_recv, stat_send, stat_recv, o_sem, oml_sem,
):
    ctx = lax.axis_index("ctx")
    grp = lax.axis_index("grp")
    place = ctx // 4
    y = (ctx // 2) % 2
    core = ctx % 2
    sibling = (ctx + 1 - 2 * core, grp)
    partner = (ctx + 2 - 4 * y, grp)
    z, x = place // 4, place % 4
    along_x = core == 0

    def at(other_place):
        return (other_place * 4 + y * 2 + core, grp)

    through = jnp.where(along_x, z < 3, z > 0)

    def mates(step):
        for dx in (1, 3, 2):
            mate = (x + dx) % 4
            step(mate, jnp.logical_or(through, mate > x), jnp.logical_or(through, mate < x))

    k_get = pltpu.make_async_copy(k_in, blocks.at[place, pl.ds(0, ROWS)], in_sem.at[0])
    v_get = pltpu.make_async_copy(v_in, v_own, in_sem.at[1])
    q_get = pltpu.make_async_copy(q_in, q_sets.at[0], in_sem.at[2])
    v_get.start()
    k_get.start()
    q_get.start()

    barrier = pltpu.get_barrier_semaphore()
    pl.semaphore_signal(barrier, inc=1, device_id=sibling, device_id_type=MESH)
    pl.semaphore_signal(barrier, inc=1, device_id=partner, device_id_type=MESH)

    def greet(mate, _, hears):
        @pl.when(hears)
        def _():
            pl.semaphore_signal(barrier, inc=1, device_id=at(z * 4 + mate), device_id_type=MESH)

    mates(greet)
    for below in range(3):
        @pl.when(below < z)
        def _(below=below):
            pl.semaphore_signal(barrier, inc=1, device_id=at(below * 4 + x), device_id_type=MESH)

    ml_ref[:, :8] = jnp.full((SETS, 8, COLS), LOW, F32)
    ml_ref[:, 8:] = jnp.zeros((SETS, 8, COLS), F32)
    acc[...] = jnp.zeros(acc.shape, F32)

    v_get.wait()
    v_t = jnp.transpose(v_own[...].astype(F32)).astype(BF16)
    blocks[place, ROWS : ROWS + HD] = v_t[:, :HD]
    blocks[place, ROWS + HD :] = v_t[:, HD:]
    k_get.wait()
    q_get.wait()

    pl.semaphore_wait(barrier, 5 - z + jnp.where(through, 3, 3 - x))

    def copy(src, dst, send, recv, device):
        return pltpu.make_async_remote_copy(
            src_ref=src, dst_ref=dst, send_sem=send, recv_sem=recv,
            device_id=device, device_id_type=MESH,
        )

    def along_x_copy(plane, mate):
        here = plane * 4 + x
        return copy(blocks.at[here], blocks.at[here], x_sem.at[plane, mate], from_sem.at[here], at(z * 4 + mate))

    def along_z_copy(column, above):
        here = z * 4 + column
        return copy(blocks.at[here], blocks.at[here], z_sem.at[column, above], from_sem.at[here], at(above * 4 + x))

    def wait_block(here):
        copy(blocks.at[here], blocks.at[here], x_sem.at[0, 0], from_sem.at[here], sibling).wait_recv()

    def up(column, step):
        for dz in (1, 2, 3):
            @pl.when(z + dz < 4)
            def _(dz=dz):
                step(along_z_copy(column, z + dz))

    def across(plane, step):
        for dx in (1, 3, 2):
            step(along_x_copy(plane, (x + dx) % 4))

    def own_across(step):
        for dx in (1, 3, 2):
            mate = (x + dx) % 4

            @pl.when(jnp.logical_or(jnp.logical_and(along_x, z < 3), mate > x))
            def _(mate=mate):
                step(along_x_copy(z, mate))

    def start(c):
        c.start()

    def gone(c):
        c.wait_send()

    q_to_sibling = copy(q_sets.at[0], q_sets.at[1], q_send.at[0], q_recv.at[0], sibling)
    q_to_partner = copy(q_sets.at[0], q_sets.at[2], q_send.at[1], q_recv.at[1], partner)
    q_passed = copy(q_sets.at[2], q_sets.at[3], q_send.at[2], q_recv.at[2], sibling)

    q_to_partner.start()
    q_to_sibling.start()

    @pl.when(core == 0)
    def _():
        own_across(start)
        up(x, start)

    @pl.when(core == 1)
    def _():
        up(x, start)
        own_across(start)

    scale = math.log2(math.e) / math.sqrt(HD)

    def ready_queries(s):
        for h in range(HEADS):
            full = jnp.transpose(q_sets[s, :, h * HD : (h + 1) * HD].astype(F32)) * scale
            hi = full.astype(BF16)
            q_t[s, :HD, h * ROWS : (h + 1) * ROWS] = hi
            q_t[s, HD:, h * ROWS : (h + 1) * ROWS] = (full - hi.astype(F32)).astype(BF16)

    s_refs, p_refs, al_refs = (s_a, s_b), (p_a, p_b), (al_a, al_b)

    def keys(plane, count):
        k = jnp.concatenate([blocks[plane * 4 + i, :ROWS] for i in range(count)], 0)
        return jnp.concatenate([k, k], 1)

    def values(plane, count):
        tiles = []
        for i in range(count):
            tiles.append(blocks[plane * 4 + i, ROWS : ROWS + HD])
            tiles.append(blocks[plane * 4 + i, ROWS + HD :])
        return jnp.concatenate(tiles, 1)

    def cols(h):
        return slice(h * ROWS, (h + 1) * ROWS)

    def scores(s, k, h, slot):
        s_refs[slot][: k.shape[0]] = dot(k, q_t[s, :, cols(h)])

    def weigh(s, h, slot, n, visible):
        score = s_refs[slot][:n]
        if visible is not None:
            score = jnp.where(visible, score, LOW)
        old = ml_ref[s, :8, cols(h)]
        top = jnp.max(score.reshape(n // 8, 8, ROWS), axis=0)
        new = jnp.maximum(old, jnp.max(top, axis=0, keepdims=True))
        w = jnp.exp2(score - new[:1])
        if visible is not None:
            w = jnp.where(visible, w, 0.0)
        alpha = jnp.exp2(old - new)
        ml_ref[s, 8:, cols(h)] = ml_ref[s, 8:, cols(h)] * alpha + jnp.sum(w.reshape(n // 8, 8, ROWS), axis=0)
        p_refs[slot][:n] = w.astype(BF16)
        al_refs[slot][...] = alpha
        ml_ref[s, :8, cols(h)] = new

    def gather(s, v, h, slot):
        acc[s, :, cols(h)] = acc[s, :, cols(h)] * al_refs[slot][:1] + dot(v, p_refs[slot][: v.shape[1]])

    def tiles(list_of, visible=None, after_set=None):
        s, h, k, v = list_of[0]
        scores(s, k, h, 0)
        for n, (s, h, k, v) in enumerate(list_of):
            if n + 1 < len(list_of):
                s_next, h_next, k_next, _ = list_of[n + 1]
                scores(s_next, k_next, h_next, (n + 1) % 2)
            if n > 0:
                s_last, h_last, _, v_last = list_of[n - 1]
                gather(s_last, v_last, h_last, (n - 1) % 2)
            weigh(s, h, n % 2, k.shape[0], visible)
            if n == HEADS and after_set is not None:
                after_set()
        s, h, k, v = list_of[-1]
        gather(s, v, h, (len(list_of) - 1) % 2)

    def own_block():
        key_at = lax.broadcasted_iota(jnp.int32, (ROWS, ROWS), 0)
        query_at = lax.broadcasted_iota(jnp.int32, (ROWS, ROWS), 1)
        k = blocks[place, :ROWS]
        k = jnp.concatenate([k, k], 1)
        v = jnp.concatenate([blocks[place, ROWS : ROWS + HD], blocks[place, ROWS + HD :]], 1)
        tiles([(0, h, k, v) for h in range(HEADS)], key_at <= query_at)

    def own_plane(s):
        set_at = jnp.where(s < 2, y, 1 - y) * 2 + jnp.where(s % 2 == 0, core, 1 - core)
        seen = x + jnp.where(set_at > y * 2 + core, 1, 0)
        for count in (1, 2, 3, 4):
            @pl.when(seen == count)
            def _(count=count):
                k, v = keys(z, count), values(z, count)
                tiles([(s, h, k, v) for h in range(HEADS)])

    def relay(step_up, step_across):
        @pl.when(core == 0)
        def _():
            for dx in (1, 3, 2):
                mate = (x + dx) % 4

                @pl.when(jnp.logical_or(through, mate < x))
                def _(mate=mate):
                    step_up(mate)

        @pl.when(core == 1)
        def _():
            for dz in (1, 2, 3):
                @pl.when(z >= dz)
                def _(dz=dz):
                    step_across(z - dz)

    def relay_up(mate):
        wait_block(z * 4 + mate)
        up(mate, start)

    def relay_across(plane):
        wait_block(plane * 4 + x)
        across(plane, start)

    def plane_at(t):
        plane = z - 1 - t
        return jnp.where(jnp.logical_and(z == 3, plane < 2), 1 - plane, plane)

    def arrive(plane):
        for column in range(4):
            @pl.when(jnp.logical_or(along_x, x != column))
            def _(column=column):
                wait_block(plane * 4 + column)

    def hand_over(s, slot):
        return (
            copy(acc.at[s], got_acc.at[slot], acc_send.at[slot], acc_recv.at[slot], sibling),
            copy(ml_ref.at[s], got_ml.at[slot], stat_send.at[slot], stat_recv.at[slot], sibling),
        )

    def merged(s, slot):
        m, l = ml_ref[s, 0:1], jnp.sum(ml_ref[s, 8:], axis=0, keepdims=True)
        m_got, l_got = got_ml[slot, 0:1], jnp.sum(got_ml[slot, 8:], axis=0, keepdims=True)
        top = jnp.maximum(m, m_got)
        f, f_got = jnp.exp2(m - top), jnp.exp2(m_got - top)
        total = l * f + l_got * f_got
        return top, total, f, f_got

    ready_queries(0)
    own_block()
    relay(relay_up, relay_across)

    @pl.when(core == 1)
    def _():
        for column in range(3):
            @pl.when(column < x)
            def _(column=column):
                wait_block(z * 4 + column)

    def plane_step(s, _):
        @pl.when(s == 1)
        def _():
            q_to_sibling.wait_recv()

        @pl.when(s == 2)
        def _():
            q_to_partner.wait_recv()
            q_passed.start()

        @pl.when(s == 3)
        def _():
            q_passed.wait_recv()

        @pl.when(s > 0)
        def _():
            ready_queries(s)

        own_plane(s)
        return 0

    lax.fori_loop(0, SETS, plane_step, 0)

    def give():
        for c in hand_over(3, 0):
            c.start()

    @pl.when(z == 0)
    def _():
        give()

    def other_layer(t, _):
        plane = plane_at(t)
        arrive(plane)
        k, v = keys(plane, 4), values(plane, 4)

        def done():
            @pl.when(t == z - 1)
            def _():
                give()

        tiles([(s, h, k, v) for s in (3, 2) for h in range(HEADS)], after_set=done)
        return 0

    lax.fori_loop(0, z, other_layer, 0)

    def own_layer(s, lo, hi):
        @pl.when(lo < hi)
        def _():
            scores(s, keys(plane_at(lo), 4), 0, 0)
            p_b[...] = jnp.zeros(p_b.shape, BF16)
            al_b[...] = jnp.ones(al_b.shape, F32)

            def step(t, _):
                k, v = keys(plane_at(t), 4), values(plane_at(t), 4)
                k_next = keys(plane_at(jnp.minimum(t + 1, hi - 1)), 4)
                v_last = values(plane_at(jnp.maximum(t - 1, lo)), 4)
                for h in range(HEADS):
                    if h + 1 < HEADS:
                        scores(s, k, h + 1, (h + 1) % 2)
                    else:
                        scores(s, k_next, 0, 0)
                    if h > 0:
                        gather(s, v, h - 1, (h - 1) % 2)
                    else:
                        gather(s, v_last, HEADS - 1, 1)
                    weigh(s, h, h % 2, KEYS, None)
                return 0

            lax.fori_loop(lo, hi, step, 0)
            gather(s, values(plane_at(hi - 1), 4), HEADS - 1, 1)

    first = jnp.minimum(z, 1)
    own_layer(1, 0, first)

    for c in hand_over(3, 0):
        c.wait_recv()
    top, total, f, f_got = merged(2, 0)
    part_ml[0:1] = top
    part_ml[1:2] = total
    part_ml[2:] = jnp.zeros((6, COLS), F32)
    safe = 1.0 / jnp.where(total > 0, total, 1.0)
    part_o[...] = (acc[2] * (f * safe) + got_acc[0] * (f_got * safe)).astype(BF16)
    o_copy = copy(part_o, got_o, o_sem.at[0], o_sem.at[1], partner)
    oml_copy = copy(part_ml, got_oml, oml_sem.at[0], oml_sem.at[1], partner)
    o_copy.start()
    oml_copy.start()

    own_layer(1, first, z)
    for c in hand_over(1, 1):
        c.start()
    own_layer(0, 0, z)

    for c in hand_over(1, 1):
        c.wait_recv()
    m_own, total, f, f_got = merged(0, 1)
    o_copy.wait_recv()
    oml_copy.wait_recv()
    m_got = got_oml[0:1]
    top = jnp.maximum(m_own, m_got)
    a_own = jnp.exp2(m_own - top)
    a_got = jnp.exp2(m_got - top) * got_oml[1:2]
    inv = 1.0 / (total * a_own + a_got)
    f, f_got, f_far = f * (a_own * inv), f_got * (a_own * inv), a_got * inv
    for h in range(HEADS):
        o = acc[0, :, cols(h)] * f[:, cols(h)] + got_acc[1, :, cols(h)] * f_got[:, cols(h)]
        o = o + got_o[:, cols(h)].astype(F32) * f_far[:, cols(h)]
        out_ref[:, h * HD : (h + 1) * HD] = jnp.transpose(o).astype(BF16)

    for c in (q_to_sibling, q_to_partner, q_passed, o_copy, oml_copy) + hand_over(3, 0) + hand_over(1, 1):
        c.wait_send()
    own_across(gone)
    up(x, gone)
    relay(lambda mate: up(mate, gone), lambda plane: across(plane, gone))


def per_device(queries, key_rows, value_rows):
    return pl.pallas_call(
        kernel,
        out_shape=jax.ShapeDtypeStruct((ROWS, HEADS * HD), BF16),
        in_specs=[pl.BlockSpec(memory_space=pl.ANY)] * 3,
        out_specs=pl.BlockSpec(memory_space=pltpu.VMEM),
        scratch_shapes=[
            pltpu.VMEM((PLACES, 2 * ROWS, HD), BF16),
            pltpu.VMEM((ROWS, HD), BF16),
            pltpu.VMEM((SETS, ROWS, HEADS * HD), BF16),
            pltpu.VMEM((SETS, 2 * HD, COLS), BF16),
            pltpu.VMEM((SETS, 16, COLS), F32),
            pltpu.VMEM((SETS, HD, COLS), F32),
            pltpu.VMEM((KEYS, ROWS), F32),
            pltpu.VMEM((KEYS, ROWS), F32),
            pltpu.VMEM((KEYS, ROWS), BF16),
            pltpu.VMEM((KEYS, ROWS), BF16),
            pltpu.VMEM((8, ROWS), F32),
            pltpu.VMEM((8, ROWS), F32),
            pltpu.VMEM((2, HD, COLS), F32),
            pltpu.VMEM((2, 16, COLS), F32),
            pltpu.VMEM((HD, COLS), BF16),
            pltpu.VMEM((8, COLS), F32),
            pltpu.VMEM((HD, COLS), BF16),
            pltpu.VMEM((8, COLS), F32),
            pltpu.SemaphoreType.DMA((3,)),
            pltpu.SemaphoreType.DMA((4, 4)),
            pltpu.SemaphoreType.DMA((4, 4)),
            pltpu.SemaphoreType.DMA((PLACES,)),
            pltpu.SemaphoreType.DMA((3,)),
            pltpu.SemaphoreType.DMA((3,)),
            pltpu.SemaphoreType.DMA((2,)),
            pltpu.SemaphoreType.DMA((2,)),
            pltpu.SemaphoreType.DMA((2,)),
            pltpu.SemaphoreType.DMA((2,)),
            pltpu.SemaphoreType.DMA((2,)),
            pltpu.SemaphoreType.DMA((2,)),
        ],
        compiler_params=pltpu.CompilerParams(
            collective_id=0, has_side_effects=True, vmem_limit_bytes=60 << 20
        ),
        name="attend",
    )(queries, key_rows, value_rows)


def solution(mesh):
    placed = (P("ctx", "grp"), P("ctx", "grp"), P("ctx", "grp"))
    return jax.shard_map(
        per_device, mesh=mesh, in_specs=placed, out_specs=P("ctx", "grp"), check_vma=False
    )
```

```python
import math

import jax
import jax.numpy as jnp
from jax import lax
from jax.experimental import pallas as pl
from jax.experimental.pallas import tpu as pltpu
from jax.sharding import PartitionSpec as P

MESH = pl.DeviceIdType.MESH
F32 = jnp.float32
BF16 = jnp.bfloat16
LOW = -1e30
ROWS = 256
HD = 128
HEADS = 4
COLS = ROWS * HEADS
PLACES = 16
KEYS = 4 * ROWS
SETS = 4
HELP = 4
EXTRA = 3


def dot(a, b):
    return lax.dot_general(a, b, (((1,), (0,)), ((), ())), preferred_element_type=F32)


def kernel(
    q_in, k_in, v_in, out_ref,
    blocks, v_own, q_sets, q_t, ml_ref, acc, s_a, s_b, p_a, p_b, al_a, al_b,
    got_acc, got_ml, part_o, part_ml, got_o, got_oml, part_h, part_hml, got_h, got_hml,
    in_sem, x_sem, z_sem, from_sem, q_send, q_recv, acc_send, acc_recv, stat_send, stat_recv, o_sem, oml_sem,
    share_send, qh_sem, h_sem, hml_sem,
):
    ctx = lax.axis_index("ctx")
    grp = lax.axis_index("grp")
    place = ctx // 4
    y = (ctx // 2) % 2
    core = ctx % 2
    sibling = (ctx + 1 - 2 * core, grp)
    partner = (ctx + 2 - 4 * y, grp)
    z, x = place // 4, place % 4
    along_x = core == 0

    def at(other_place):
        return (other_place * 4 + y * 2 + core, grp)

    through = jnp.logical_or(jnp.logical_not(along_x), z < 3)
    helped = at(12 + x)
    helper = at(x)

    def mates(step):
        for dx in (1, 3, 2):
            mate = (x + dx) % 4
            step(mate, jnp.logical_or(through, mate > x), jnp.logical_or(through, mate < x))

    k_get = pltpu.make_async_copy(k_in, blocks.at[place, pl.ds(0, ROWS)], in_sem.at[0])
    v_get = pltpu.make_async_copy(v_in, v_own, in_sem.at[1])
    q_get = pltpu.make_async_copy(q_in, q_sets.at[0], in_sem.at[2])
    v_get.start()
    k_get.start()
    q_get.start()

    barrier = pltpu.get_barrier_semaphore()
    pl.semaphore_signal(barrier, inc=1, device_id=sibling, device_id_type=MESH)
    pl.semaphore_signal(barrier, inc=1, device_id=partner, device_id_type=MESH)

    def greet(mate, _, hears):
        @pl.when(hears)
        def _():
            pl.semaphore_signal(barrier, inc=1, device_id=at(z * 4 + mate), device_id_type=MESH)

    mates(greet)
    for below in range(3):
        @pl.when(below < z)
        def _(below=below):
            pl.semaphore_signal(barrier, inc=1, device_id=at(below * 4 + x), device_id_type=MESH)

    @pl.when(z == 0)
    def _():
        pl.semaphore_signal(barrier, inc=1, device_id=helped, device_id_type=MESH)

    ml_ref[:, :8] = jnp.full((SETS + 1, 8, COLS), LOW, F32)
    ml_ref[:, 8:] = jnp.zeros((SETS + 1, 8, COLS), F32)
    acc[...] = jnp.zeros(acc.shape, F32)

    @pl.when(z != 3)
    def _():
        got_h[...] = jnp.zeros(got_h.shape, BF16)
        got_hml[...] = jnp.full(got_hml.shape, LOW, F32)

    v_get.wait()
    v_t = jnp.transpose(v_own[...].astype(F32)).astype(BF16)
    blocks[place, ROWS : ROWS + HD] = v_t[:, :HD]
    blocks[place, ROWS + HD :] = v_t[:, HD:]
    k_get.wait()
    q_get.wait()

    pl.semaphore_wait(barrier, 5 - z + jnp.where(z == 3, 1, 0) + jnp.where(through, 3, 3 - x))

    def copy(src, dst, send, recv, device):
        return pltpu.make_async_remote_copy(
            src_ref=src, dst_ref=dst, send_sem=send, recv_sem=recv,
            device_id=device, device_id_type=MESH,
        )

    def along_x_copy(plane, mate):
        here = plane * 4 + x
        return copy(blocks.at[here], blocks.at[here], x_sem.at[plane, mate], from_sem.at[here], at(z * 4 + mate))

    def along_z_copy(column, above):
        here = z * 4 + column
        return copy(blocks.at[here], blocks.at[here], z_sem.at[column, above], from_sem.at[here], at(above * 4 + x))

    def wait_block(here):
        copy(blocks.at[here], blocks.at[here], x_sem.at[0, 0], from_sem.at[here], sibling).wait_recv()

    def up(column, step):
        for dz in (1, 2):
            @pl.when(z + dz < 4)
            def _(dz=dz):
                step(along_z_copy(column, z + dz))

    def across(plane, step):
        for dx in (1, 3, 2):
            step(along_x_copy(plane, (x + dx) % 4))

    def own_across(step):
        for dx in (1, 3, 2):
            mate = (x + dx) % 4

            @pl.when(jnp.logical_or(jnp.logical_or(jnp.logical_and(along_x, z < 3), z == 0), mate > x))
            def _(mate=mate):
                step(along_x_copy(z, mate))

    def share_copies(column):
        return (
            copy(blocks.at[column], blocks.at[16 + column], share_send.at[0, column], from_sem.at[16 + column], sibling),
            copy(blocks.at[column], blocks.at[20 + column], share_send.at[1, column], from_sem.at[20 + column], partner),
        )

    def share_pass(column):
        return copy(
            blocks.at[20 + column], blocks.at[24 + column], share_send.at[2, column], from_sem.at[24 + column], sibling
        )

    def share(column):
        @pl.when(z == 0)
        def _():
            for c in share_copies(column):
                c.start()

    def start(c):
        c.start()

    def gone(c):
        c.wait_send()

    q_to_sibling = copy(q_sets.at[0], q_sets.at[1], q_send.at[0], q_recv.at[0], sibling)
    q_to_partner = copy(q_sets.at[0], q_sets.at[2], q_send.at[1], q_recv.at[1], partner)
    q_help = copy(q_sets.at[0], q_sets.at[HELP], qh_sem.at[0], qh_sem.at[1], helper)
    h_copy = copy(part_h, got_h, h_sem.at[0], h_sem.at[1], helped)
    hml_copy = copy(part_hml, got_hml, hml_sem.at[0], hml_sem.at[1], helped)
    q_passed = copy(q_sets.at[2], q_sets.at[3], q_send.at[2], q_recv.at[2], sibling)

    q_to_sibling.start()

    @pl.when(z == 3)
    def _():
        q_help.start()

    @pl.when(core == 0)
    def _():
        own_across(start)
        up(x, start)

    @pl.when(core == 1)
    def _():
        up(x, start)
        own_across(start)

    q_to_partner.start()
    share(x)

    scale = math.log2(math.e) / math.sqrt(HD)

    def ready_queries(s):
        for h in range(HEADS):
            full = jnp.transpose(q_sets[s, :, h * HD : (h + 1) * HD].astype(F32)) * scale
            hi = full.astype(BF16)
            q_t[s, :HD, h * ROWS : (h + 1) * ROWS] = hi
            q_t[s, HD:, h * ROWS : (h + 1) * ROWS] = (full - hi.astype(F32)).astype(BF16)

    s_refs, p_refs, al_refs = (s_a, s_b), (p_a, p_b), (al_a, al_b)

    def keys(plane, count):
        k = jnp.concatenate([blocks[plane * 4 + i, :ROWS] for i in range(count)], 0)
        return jnp.concatenate([k, k], 1)

    def values(plane, count):
        tiles = []
        for i in range(count):
            tiles.append(blocks[plane * 4 + i, ROWS : ROWS + HD])
            tiles.append(blocks[plane * 4 + i, ROWS + HD :])
        return jnp.concatenate(tiles, 1)

    def cols(h):
        return slice(h * ROWS, (h + 1) * ROWS)

    def scores(s, k, h, slot):
        s_refs[slot][: k.shape[0]] = dot(k, q_t[s, :, cols(h)])

    def weigh(s, h, slot, n, visible):
        score = s_refs[slot][:n]
        if visible is not None:
            score = jnp.where(visible, score, LOW)
        old = ml_ref[s, :8, cols(h)]
        top = jnp.max(score.reshape(n // 8, 8, ROWS), axis=0)
        new = jnp.maximum(old, jnp.max(top, axis=0, keepdims=True))
        w = jnp.exp2(score - new[:1])
        if visible is not None:
            w = jnp.where(visible, w, 0.0)
        alpha = jnp.exp2(old - new)
        ml_ref[s, 8:, cols(h)] = ml_ref[s, 8:, cols(h)] * alpha + jnp.sum(w.reshape(n // 8, 8, ROWS), axis=0)
        p_refs[slot][:n] = w.astype(BF16)
        al_refs[slot][...] = alpha
        ml_ref[s, :8, cols(h)] = new

    def gather(s, v, h, slot):
        acc[s, :, cols(h)] = acc[s, :, cols(h)] * al_refs[slot][:1] + dot(v, p_refs[slot][: v.shape[1]])

    def tiles(list_of, visible=None, after_set=None):
        s, h, k, v = list_of[0]
        scores(s, k, h, 0)
        for n, (s, h, k, v) in enumerate(list_of):
            if n + 1 < len(list_of):
                s_next, h_next, k_next, _ = list_of[n + 1]
                scores(s_next, k_next, h_next, (n + 1) % 2)
            if n > 0:
                s_last, h_last, _, v_last = list_of[n - 1]
                gather(s_last, v_last, h_last, (n - 1) % 2)
            weigh(s, h, n % 2, k.shape[0], visible)
            if n == HEADS and after_set is not None:
                after_set()
        s, h, k, v = list_of[-1]
        gather(s, v, h, (len(list_of) - 1) % 2)

    def own_block():
        key_at = lax.broadcasted_iota(jnp.int32, (ROWS, ROWS), 0)
        query_at = lax.broadcasted_iota(jnp.int32, (ROWS, ROWS), 1)
        k = blocks[place, :ROWS]
        k = jnp.concatenate([k, k], 1)
        v = jnp.concatenate([blocks[place, ROWS : ROWS + HD], blocks[place, ROWS + HD :]], 1)
        tiles([(0, h, k, v) for h in range(HEADS)], key_at <= query_at)

    def own_plane(s):
        set_at = jnp.where(s < 2, y, 1 - y) * 2 + jnp.where(s % 2 == 0, core, 1 - core)
        seen = x + jnp.where(set_at > y * 2 + core, 1, 0)
        for count in (1, 2, 3, 4):
            @pl.when(seen == count)
            def _(count=count):
                k, v = keys(z, count), values(z, count)
                tiles([(s, h, k, v) for h in range(HEADS)])

    def relay(step_up, step_across):
        @pl.when(core == 0)
        def _():
            for dx in (1, 3, 2):
                mate = (x + dx) % 4

                @pl.when(jnp.logical_or(through, mate < x))
                def _(mate=mate):
                    step_up(mate)

        @pl.when(core == 1)
        def _():
            for dz in (1, 2):
                @pl.when(z >= dz)
                def _(dz=dz):
                    step_across(z - dz)

    def relay_up(mate):
        wait_block(z * 4 + mate)
        up(mate, start)
        share(mate)

    def relay_across(plane):
        wait_block(plane * 4 + x)
        across(plane, start)

    def plane_at(t):
        return z - 1 - t

    def arrive(plane):
        for column in range(4):
            @pl.when(jnp.logical_or(along_x, x != column))
            def _(column=column):
                wait_block(plane * 4 + column)

    def hand_over(s, slot):
        return (
            copy(acc.at[s], got_acc.at[slot], acc_send.at[slot], acc_recv.at[slot], sibling),
            copy(ml_ref.at[s], got_ml.at[slot], stat_send.at[slot], stat_recv.at[slot], sibling),
        )

    def merged(s, slot):
        m, l = ml_ref[s, 0:1], jnp.sum(ml_ref[s, 8:], axis=0, keepdims=True)
        m_got, l_got = got_ml[slot, 0:1], jnp.sum(got_ml[slot, 8:], axis=0, keepdims=True)
        top = jnp.maximum(m, m_got)
        f, f_got = jnp.exp2(m - top), jnp.exp2(m_got - top)
        total = l * f + l_got * f_got
        return top, total, f, f_got

    ready_queries(0)
    own_block()
    relay(relay_up, relay_across)

    @pl.when(core == 1)
    def _():
        for column in range(4):
            @pl.when(jnp.logical_or(jnp.logical_and(z == 0, column != x), column < x))
            def _(column=column):
                wait_block(z * 4 + column)
                share(column)

    def plane_step(s, _):
        @pl.when(s == 1)
        def _():
            q_to_sibling.wait_recv()

        @pl.when(s == 2)
        def _():
            q_to_partner.wait_recv()
            q_passed.start()

        @pl.when(s == 3)
        def _():
            q_passed.wait_recv()

        @pl.when(s > 0)
        def _():
            ready_queries(s)

        own_plane(s)
        return 0

    lax.fori_loop(0, SETS, plane_step, 0)

    def give():
        for c in hand_over(3, 0):
            c.start()

    @pl.when(z == 0)
    def _():
        give()

    def other_layer(t, _):
        plane = plane_at(t)
        arrive(plane)
        k, v = keys(plane, 4), values(plane, 4)

        def done():
            @pl.when(t == planes - 1)
            def _():
                give()

        tiles([(s, h, k, v) for s in (3, 2) for h in range(HEADS)], after_set=done)
        return 0

    planes = jnp.minimum(z, 2)
    lax.fori_loop(0, planes, other_layer, 0)

    def own_layer(s, lo, hi, plane_at=plane_at):
        @pl.when(lo < hi)
        def _():
            scores(s, keys(plane_at(lo), 4), 0, 0)
            p_b[...] = jnp.zeros(p_b.shape, BF16)
            al_b[...] = jnp.ones(al_b.shape, F32)

            def step(t, _):
                k, v = keys(plane_at(t), 4), values(plane_at(t), 4)
                k_next = keys(plane_at(jnp.minimum(t + 1, hi - 1)), 4)
                v_last = values(plane_at(jnp.maximum(t - 1, lo)), 4)
                for h in range(HEADS):
                    if h + 1 < HEADS:
                        scores(s, k, h + 1, (h + 1) % 2)
                    else:
                        scores(s, k_next, 0, 0)
                    if h > 0:
                        gather(s, v, h - 1, (h - 1) % 2)
                    else:
                        gather(s, v_last, HEADS - 1, 1)
                    weigh(s, h, h % 2, KEYS, None)
                return 0

            lax.fori_loop(lo, hi, step, 0)
            gather(s, values(plane_at(hi - 1), 4), HEADS - 1, 1)

    def help_at(t):
        return jnp.where(t == 0, 0, t + 3)

    @pl.when(z == 0)
    def _():
        q_help.wait_recv()
        ready_queries(HELP)
        for column in range(4):
            wait_block(16 + column)
        own_layer(HELP, 0, 2, help_at)

    first = jnp.minimum(planes, 1)
    own_layer(1, 0, first)

    for c in hand_over(3, 0):
        c.wait_recv()
    top, total, f, f_got = merged(2, 0)
    part_ml[0:1] = top
    part_ml[1:2] = total
    part_ml[2:] = jnp.zeros((6, COLS), F32)
    safe = 1.0 / jnp.where(total > 0, total, 1.0)
    part_o[...] = (acc[2] * (f * safe) + got_acc[0] * (f_got * safe)).astype(BF16)
    o_copy = copy(part_o, got_o, o_sem.at[0], o_sem.at[1], partner)
    oml_copy = copy(part_ml, got_oml, oml_sem.at[0], oml_sem.at[1], partner)
    o_copy.start()
    oml_copy.start()

    own_layer(1, first, planes)
    for c in hand_over(1, 1):
        c.start()
    own_layer(0, 0, planes)

    @pl.when(z == 0)
    def _():
        for column in range(4):
            wait_block(20 + column)
            share_pass(column).start()
        own_layer(HELP, 2, 3, help_at)
        for column in range(4):
            wait_block(24 + column)
        own_layer(HELP, 3, 4, help_at)
        l_h = jnp.sum(ml_ref[HELP, 8:], axis=0, keepdims=True)
        part_hml[0:1] = ml_ref[HELP, 0:1]
        part_hml[1:2] = l_h
        part_hml[2:] = jnp.zeros((6, COLS), F32)
        part_h[...] = (acc[HELP] * (1.0 / l_h)).astype(BF16)
        h_copy.start()
        hml_copy.start()

    for c in hand_over(1, 1):
        c.wait_recv()
    m_own, total, f, f_got = merged(0, 1)
    o_copy.wait_recv()
    oml_copy.wait_recv()

    @pl.when(z == 3)
    def _():
        h_copy.wait_recv()
        hml_copy.wait_recv()

    m_got, m_h = got_oml[0:1], got_hml[0:1]
    top = jnp.maximum(jnp.maximum(m_own, m_got), m_h)
    a_own = jnp.exp2(m_own - top)
    a_got = jnp.exp2(m_got - top) * got_oml[1:2]
    a_h = jnp.where(z == 3, jnp.exp2(m_h - top) * got_hml[1:2], 0.0)
    inv = 1.0 / (total * a_own + a_got + a_h)
    f, f_got, f_far, f_h = f * (a_own * inv), f_got * (a_own * inv), a_got * inv, a_h * inv
    for h in range(HEADS):
        o = acc[0, :, cols(h)] * f[:, cols(h)] + got_acc[1, :, cols(h)] * f_got[:, cols(h)]
        o = o + got_o[:, cols(h)].astype(F32) * f_far[:, cols(h)] + got_h[:, cols(h)].astype(F32) * f_h[:, cols(h)]
        out_ref[:, h * HD : (h + 1) * HD] = jnp.transpose(o).astype(BF16)

    for c in (q_to_sibling, q_to_partner, q_passed, o_copy, oml_copy) + hand_over(3, 0) + hand_over(1, 1):
        c.wait_send()
    own_across(gone)
    up(x, gone)

    @pl.when(z == 3)
    def _():
        q_help.wait_send()

    @pl.when(z == 0)
    def _():
        h_copy.wait_send()
        hml_copy.wait_send()
        for column in range(4):
            for c in share_copies(column) + (share_pass(column),):
                c.wait_send()

    relay(lambda mate: up(mate, gone), lambda plane: across(plane, gone))


def per_device(queries, key_rows, value_rows):
    return pl.pallas_call(
        kernel,
        out_shape=jax.ShapeDtypeStruct((ROWS, HEADS * HD), BF16),
        in_specs=[pl.BlockSpec(memory_space=pl.ANY)] * 3,
        out_specs=pl.BlockSpec(memory_space=pltpu.VMEM),
        scratch_shapes=[
            pltpu.VMEM((PLACES + 4 * EXTRA, 2 * ROWS, HD), BF16),
            pltpu.VMEM((ROWS, HD), BF16),
            pltpu.VMEM((SETS + 1, ROWS, HEADS * HD), BF16),
            pltpu.VMEM((SETS + 1, 2 * HD, COLS), BF16),
            pltpu.VMEM((SETS + 1, 16, COLS), F32),
            pltpu.VMEM((SETS + 1, HD, COLS), F32),
            pltpu.VMEM((KEYS, ROWS), F32),
            pltpu.VMEM((KEYS, ROWS), F32),
            pltpu.VMEM((KEYS, ROWS), BF16),
            pltpu.VMEM((KEYS, ROWS), BF16),
            pltpu.VMEM((8, ROWS), F32),
            pltpu.VMEM((8, ROWS), F32),
            pltpu.VMEM((2, HD, COLS), F32),
            pltpu.VMEM((2, 16, COLS), F32),
            pltpu.VMEM((HD, COLS), BF16),
            pltpu.VMEM((8, COLS), F32),
            pltpu.VMEM((HD, COLS), BF16),
            pltpu.VMEM((8, COLS), F32),
            pltpu.VMEM((HD, COLS), BF16),
            pltpu.VMEM((8, COLS), F32),
            pltpu.VMEM((HD, COLS), BF16),
            pltpu.VMEM((8, COLS), F32),
            pltpu.SemaphoreType.DMA((3,)),
            pltpu.SemaphoreType.DMA((4, 4)),
            pltpu.SemaphoreType.DMA((4, 4)),
            pltpu.SemaphoreType.DMA((PLACES + 4 * EXTRA,)),
            pltpu.SemaphoreType.DMA((3,)),
            pltpu.SemaphoreType.DMA((3,)),
            pltpu.SemaphoreType.DMA((2,)),
            pltpu.SemaphoreType.DMA((2,)),
            pltpu.SemaphoreType.DMA((2,)),
            pltpu.SemaphoreType.DMA((2,)),
            pltpu.SemaphoreType.DMA((2,)),
            pltpu.SemaphoreType.DMA((2,)),
            pltpu.SemaphoreType.DMA((3, 4)),
            pltpu.SemaphoreType.DMA((2,)),
            pltpu.SemaphoreType.DMA((2,)),
            pltpu.SemaphoreType.DMA((2,)),
        ],
        compiler_params=pltpu.CompilerParams(
            collective_id=0, has_side_effects=True, vmem_limit_bytes=60 << 20
        ),
        name="attend",
    )(queries, key_rows, value_rows)


def solution(mesh):
    placed = (P("ctx", "grp"), P("ctx", "grp"), P("ctx", "grp"))
    return jax.shard_map(
        per_device, mesh=mesh, in_specs=placed, out_specs=P("ctx", "grp"), check_vma=False
    )
```

```python
import math

import jax
import jax.numpy as jnp
from jax import lax
from jax.experimental import pallas as pl
from jax.experimental.pallas import tpu as pltpu
from jax.sharding import PartitionSpec as P

MESH = pl.DeviceIdType.MESH
F32 = jnp.float32
BF16 = jnp.bfloat16
LOW = -1e30
ROWS = 256
HD = 128
HEADS = 4
COLS = ROWS * HEADS
PLACES = 16
KEYS = 4 * ROWS
SETS = 4
HELP = 4
EXTRA = 3


def dot(a, b):
    return lax.dot_general(a, b, (((1,), (0,)), ((), ())), preferred_element_type=F32)


def kernel(
    q_in, k_in, v_in, out_ref,
    blocks, v_own, q_sets, q_t, ml_ref, acc, s_a, s_b, p_a, p_b, al_a, al_b,
    got_acc, got_ml, part_o, part_ml, got_o, got_oml, part_h, part_hml, got_h, got_hml,
    in_sem, x_sem, z_sem, from_sem, q_send, q_recv, acc_send, acc_recv, stat_send, stat_recv, o_sem, oml_sem,
    share_send, qh_sem, h_sem, hml_sem,
):
    ctx = lax.axis_index("ctx")
    grp = lax.axis_index("grp")
    place = ctx // 4
    y = (ctx // 2) % 2
    core = ctx % 2
    sibling = (ctx + 1 - 2 * core, grp)
    partner = (ctx + 2 - 4 * y, grp)
    z, x = place // 4, place % 4
    along_x = core == 0

    def at(other_place):
        return (other_place * 4 + y * 2 + core, grp)

    through = jnp.logical_or(jnp.logical_not(along_x), z < 3)
    helped = at(12 + x)
    helper = at(x)

    def mates(step):
        for dx in (1, 3, 2):
            mate = (x + dx) % 4
            step(mate, jnp.logical_or(through, mate > x), jnp.logical_or(through, mate < x))

    k_get = pltpu.make_async_copy(k_in, blocks.at[place, pl.ds(0, ROWS)], in_sem.at[0])
    v_get = pltpu.make_async_copy(v_in, v_own, in_sem.at[1])
    q_get = pltpu.make_async_copy(q_in, q_sets.at[0], in_sem.at[2])
    v_get.start()
    k_get.start()
    q_get.start()

    barrier = pltpu.get_barrier_semaphore()
    pl.semaphore_signal(barrier, inc=1, device_id=sibling, device_id_type=MESH)
    pl.semaphore_signal(barrier, inc=1, device_id=partner, device_id_type=MESH)

    def greet(mate, _, hears):
        @pl.when(hears)
        def _():
            pl.semaphore_signal(barrier, inc=1, device_id=at(z * 4 + mate), device_id_type=MESH)

    mates(greet)
    for below in range(3):
        @pl.when(below < z)
        def _(below=below):
            pl.semaphore_signal(barrier, inc=1, device_id=at(below * 4 + x), device_id_type=MESH)

    @pl.when(z == 0)
    def _():
        pl.semaphore_signal(barrier, inc=1, device_id=helped, device_id_type=MESH)

    ml_ref[:, :8] = jnp.full((SETS + 1, 8, COLS), LOW, F32)
    ml_ref[:, 8:] = jnp.zeros((SETS + 1, 8, COLS), F32)
    acc[...] = jnp.zeros(acc.shape, F32)

    @pl.when(z != 3)
    def _():
        got_h[...] = jnp.zeros(got_h.shape, BF16)
        got_hml[...] = jnp.full(got_hml.shape, LOW, F32)

    v_get.wait()
    v_t = jnp.transpose(v_own[...].astype(F32)).astype(BF16)
    blocks[place, ROWS : ROWS + HD] = v_t[:, :HD]
    blocks[place, ROWS + HD :] = v_t[:, HD:]
    k_get.wait()
    q_get.wait()

    pl.semaphore_wait(barrier, 5 - z + jnp.where(z == 3, 1, 0) + jnp.where(through, 3, 3 - x))

    def copy(src, dst, send, recv, device):
        return pltpu.make_async_remote_copy(
            src_ref=src, dst_ref=dst, send_sem=send, recv_sem=recv,
            device_id=device, device_id_type=MESH,
        )

    def along_x_copy(plane, mate):
        here = plane * 4 + x
        return copy(blocks.at[here], blocks.at[here], x_sem.at[plane, mate], from_sem.at[here], at(z * 4 + mate))

    def along_z_copy(column, above):
        here = z * 4 + column
        return copy(blocks.at[here], blocks.at[here], z_sem.at[column, above], from_sem.at[here], at(above * 4 + x))

    def wait_block(here):
        copy(blocks.at[here], blocks.at[here], x_sem.at[0, 0], from_sem.at[here], sibling).wait_recv()

    def up(column, step):
        for dz in (1, 2):
            @pl.when(z + dz < 4)
            def _(dz=dz):
                step(along_z_copy(column, z + dz))

    def across(plane, step):
        for dx in (1, 3, 2):
            step(along_x_copy(plane, (x + dx) % 4))

    def own_across(step):
        for dx in (1, 3, 2):
            mate = (x + dx) % 4

            @pl.when(jnp.logical_or(jnp.logical_or(jnp.logical_and(along_x, z < 3), z == 0), mate > x))
            def _(mate=mate):
                step(along_x_copy(z, mate))

    def share_copies(column):
        return (
            copy(blocks.at[column], blocks.at[16 + column], share_send.at[0, column], from_sem.at[16 + column], sibling),
            copy(blocks.at[column], blocks.at[20 + column], share_send.at[1, column], from_sem.at[20 + column], partner),
        )

    def share_pass(column):
        return copy(
            blocks.at[20 + column], blocks.at[24 + column], share_send.at[2, column], from_sem.at[24 + column], sibling
        )

    def share(column):
        @pl.when(z == 0)
        def _():
            for c in share_copies(column):
                c.start()

    def start(c):
        c.start()

    def gone(c):
        c.wait_send()

    q_to_sibling = copy(q_sets.at[0], q_sets.at[1], q_send.at[0], q_recv.at[0], sibling)
    q_to_partner = copy(q_sets.at[0], q_sets.at[2], q_send.at[1], q_recv.at[1], partner)
    q_help = copy(q_sets.at[0], q_sets.at[HELP], qh_sem.at[0], qh_sem.at[1], helper)
    h_copy = copy(part_h, got_h, h_sem.at[0], h_sem.at[1], helped)
    hml_copy = copy(part_hml, got_hml, hml_sem.at[0], hml_sem.at[1], helped)
    q_passed = copy(q_sets.at[2], q_sets.at[3], q_send.at[2], q_recv.at[2], sibling)

    q_to_sibling.start()

    @pl.when(core == 0)
    def _():
        own_across(start)

    @pl.when(core == 1)
    def _():
        up(x, start)

    q_to_partner.start()

    @pl.when(core == 0)
    def _():
        up(x, start)

    @pl.when(core == 1)
    def _():
        own_across(start)

    @pl.when(z == 3)
    def _():
        q_help.start()

    share(x)

    scale = math.log2(math.e) / math.sqrt(HD)

    def ready_queries(s):
        for h in range(HEADS):
            full = jnp.transpose(q_sets[s, :, h * HD : (h + 1) * HD].astype(F32)) * scale
            hi = full.astype(BF16)
            q_t[s, :HD, h * ROWS : (h + 1) * ROWS] = hi
            q_t[s, HD:, h * ROWS : (h + 1) * ROWS] = (full - hi.astype(F32)).astype(BF16)

    s_refs, p_refs, al_refs = (s_a, s_b), (p_a, p_b), (al_a, al_b)

    def keys(plane, count):
        k = jnp.concatenate([blocks[plane * 4 + i, :ROWS] for i in range(count)], 0)
        return jnp.concatenate([k, k], 1)

    def values(plane, count):
        tiles = []
        for i in range(count):
            tiles.append(blocks[plane * 4 + i, ROWS : ROWS + HD])
            tiles.append(blocks[plane * 4 + i, ROWS + HD :])
        return jnp.concatenate(tiles, 1)

    def cols(h):
        return slice(h * ROWS, (h + 1) * ROWS)

    def scores(s, k, h, slot):
        s_refs[slot][: k.shape[0]] = dot(k, q_t[s, :, cols(h)])

    def weigh(s, h, slot, n, visible):
        score = s_refs[slot][:n]
        if visible is not None:
            score = jnp.where(visible, score, LOW)
        old = ml_ref[s, :8, cols(h)]
        top = jnp.max(score.reshape(n // 8, 8, ROWS), axis=0)
        new = jnp.maximum(old, jnp.max(top, axis=0, keepdims=True))
        w = jnp.exp2(score - new[:1])
        if visible is not None:
            w = jnp.where(visible, w, 0.0)
        alpha = jnp.exp2(old - new)
        ml_ref[s, 8:, cols(h)] = ml_ref[s, 8:, cols(h)] * alpha + jnp.sum(w.reshape(n // 8, 8, ROWS), axis=0)
        p_refs[slot][:n] = w.astype(BF16)
        al_refs[slot][...] = alpha
        ml_ref[s, :8, cols(h)] = new

    def gather(s, v, h, slot):
        acc[s, :, cols(h)] = acc[s, :, cols(h)] * al_refs[slot][:1] + dot(v, p_refs[slot][: v.shape[1]])

    def tiles(list_of, visible=None):
        s, h, k, v = list_of[0]
        scores(s, k, h, 0)
        for n, (s, h, k, v) in enumerate(list_of):
            if n + 1 < len(list_of):
                s_next, h_next, k_next, _ = list_of[n + 1]
                scores(s_next, k_next, h_next, (n + 1) % 2)
            if n > 0:
                s_last, h_last, _, v_last = list_of[n - 1]
                gather(s_last, v_last, h_last, (n - 1) % 2)
            weigh(s, h, n % 2, k.shape[0], visible)
        s, h, k, v = list_of[-1]
        gather(s, v, h, (len(list_of) - 1) % 2)

    def own_block():
        key_at = lax.broadcasted_iota(jnp.int32, (ROWS, ROWS), 0)
        query_at = lax.broadcasted_iota(jnp.int32, (ROWS, ROWS), 1)
        k = blocks[place, :ROWS]
        k = jnp.concatenate([k, k], 1)
        v = jnp.concatenate([blocks[place, ROWS : ROWS + HD], blocks[place, ROWS + HD :]], 1)
        tiles([(0, h, k, v) for h in range(HEADS)], key_at <= query_at)

    def own_plane(s):
        set_at = jnp.where(s < 2, y, 1 - y) * 2 + jnp.where(s % 2 == 0, core, 1 - core)
        seen = x + jnp.where(set_at > y * 2 + core, 1, 0)
        for count in (1, 2, 3, 4):
            @pl.when(seen == count)
            def _(count=count):
                k, v = keys(z, count), values(z, count)
                tiles([(s, h, k, v) for h in range(HEADS)])

    def relay(step_up, step_across):
        @pl.when(core == 0)
        def _():
            for dx in (1, 3, 2):
                mate = (x + dx) % 4

                @pl.when(jnp.logical_or(through, mate < x))
                def _(mate=mate):
                    step_up(mate)

        @pl.when(core == 1)
        def _():
            for dz in (1, 2):
                @pl.when(z >= dz)
                def _(dz=dz):
                    step_across(z - dz)

    def relay_up(mate):
        wait_block(z * 4 + mate)
        up(mate, start)
        share(mate)

    def relay_across(plane):
        wait_block(plane * 4 + x)
        across(plane, start)

    def plane_at(t):
        return z - 1 - t

    def arrive(plane):
        for column in range(4):
            @pl.when(jnp.logical_or(along_x, x != column))
            def _(column=column):
                wait_block(plane * 4 + column)

    def hand_over(s, slot):
        return (
            copy(acc.at[s], got_acc.at[slot], acc_send.at[slot], acc_recv.at[slot], sibling),
            copy(ml_ref.at[s], got_ml.at[slot], stat_send.at[slot], stat_recv.at[slot], sibling),
        )

    def merged(s, slot):
        m, l = ml_ref[s, 0:1], jnp.sum(ml_ref[s, 8:], axis=0, keepdims=True)
        m_got, l_got = got_ml[slot, 0:1], jnp.sum(got_ml[slot, 8:], axis=0, keepdims=True)
        top = jnp.maximum(m, m_got)
        f, f_got = jnp.exp2(m - top), jnp.exp2(m_got - top)
        total = l * f + l_got * f_got
        return top, total, f, f_got

    ready_queries(0)
    own_block()
    q_to_sibling.wait_recv()
    ready_queries(1)
    relay(relay_up, relay_across)

    @pl.when(core == 1)
    def _():
        for column in range(4):
            @pl.when(jnp.logical_or(jnp.logical_and(z == 0, column != x), column < x))
            def _(column=column):
                wait_block(z * 4 + column)
                share(column)

    def plane_step(t, _):
        s = t + 1

        @pl.when(s == 2)
        def _():
            q_to_partner.wait_recv()
            q_passed.start()

        @pl.when(s == 3)
        def _():
            q_passed.wait_recv()

        @pl.when(s > 1)
        def _():
            ready_queries(s)

        own_plane(s)
        return 0

    lax.fori_loop(0, 3, plane_step, 0)

    def layers(s, lo, hi, plane_at=plane_at):
        @pl.when(lo < hi)
        def _():
            scores(s, keys(plane_at(lo), 4), 0, 0)
            p_b[...] = jnp.zeros(p_b.shape, BF16)
            al_b[...] = jnp.ones(al_b.shape, F32)

            def step(t, _):
                k, v = keys(plane_at(t), 4), values(plane_at(t), 4)
                k_next = keys(plane_at(jnp.minimum(t + 1, hi - 1)), 4)
                v_last = values(plane_at(jnp.maximum(t - 1, lo)), 4)
                for h in range(HEADS):
                    if h + 1 < HEADS:
                        scores(s, k, h + 1, (h + 1) % 2)
                    else:
                        scores(s, k_next, 0, 0)
                    if h > 0:
                        gather(s, v, h - 1, (h - 1) % 2)
                    else:
                        gather(s, v_last, HEADS - 1, 1)
                    weigh(s, h, h % 2, KEYS, None)
                return 0

            lax.fori_loop(lo, hi, step, 0)
            gather(s, values(plane_at(hi - 1), 4), HEADS - 1, 1)

    planes = jnp.minimum(z, 2)

    def siblings_partner(t, _):
        plane = plane_at(t)
        arrive(plane)
        k, v = keys(plane, 4), values(plane, 4)
        tiles([(3, h, k, v) for h in range(HEADS)])
        return 0

    lax.fori_loop(0, planes, siblings_partner, 0)
    for c in hand_over(3, 0):
        c.start()
    layers(2, 0, planes)

    def help_at(t):
        return jnp.where(t == 0, 0, t + 3)

    @pl.when(z == 0)
    def _():
        q_help.wait_recv()
        ready_queries(HELP)
        for column in range(4):
            wait_block(16 + column)
        layers(HELP, 0, 2, help_at)


    for c in hand_over(3, 0):
        c.wait_recv()
    top, total, f, f_got = merged(2, 0)
    part_ml[0:1] = top
    part_ml[1:2] = total
    part_ml[2:] = jnp.zeros((6, COLS), F32)
    safe = 1.0 / jnp.where(total > 0, total, 1.0)
    part_o[...] = (acc[2] * (f * safe) + got_acc[0] * (f_got * safe)).astype(BF16)
    o_copy = copy(part_o, got_o, o_sem.at[0], o_sem.at[1], partner)
    oml_copy = copy(part_ml, got_oml, oml_sem.at[0], oml_sem.at[1], partner)
    o_copy.start()
    oml_copy.start()

    layers(1, 0, planes)
    for c in hand_over(1, 1):
        c.start()
    own_plane(0)
    layers(0, 0, planes)

    @pl.when(z == 0)
    def _():
        for column in range(4):
            wait_block(20 + column)
            share_pass(column).start()
        layers(HELP, 2, 3, help_at)
        for column in range(4):
            wait_block(24 + column)
        layers(HELP, 3, 4, help_at)
        l_h = jnp.sum(ml_ref[HELP, 8:], axis=0, keepdims=True)
        part_hml[0:1] = ml_ref[HELP, 0:1]
        part_hml[1:2] = l_h
        part_hml[2:] = jnp.zeros((6, COLS), F32)
        part_h[...] = (acc[HELP] * (1.0 / l_h)).astype(BF16)
        h_copy.start()
        hml_copy.start()

    for c in hand_over(1, 1):
        c.wait_recv()
    m_own, total, f, f_got = merged(0, 1)
    o_copy.wait_recv()
    oml_copy.wait_recv()

    @pl.when(z == 3)
    def _():
        h_copy.wait_recv()
        hml_copy.wait_recv()

    m_got, m_h = got_oml[0:1], got_hml[0:1]
    top = jnp.maximum(jnp.maximum(m_own, m_got), m_h)
    a_own = jnp.exp2(m_own - top)
    a_got = jnp.exp2(m_got - top) * got_oml[1:2]
    a_h = jnp.where(z == 3, jnp.exp2(m_h - top) * got_hml[1:2], 0.0)
    inv = 1.0 / (total * a_own + a_got + a_h)
    f, f_got, f_far, f_h = f * (a_own * inv), f_got * (a_own * inv), a_got * inv, a_h * inv
    for h in range(HEADS):
        o = acc[0, :, cols(h)] * f[:, cols(h)] + got_acc[1, :, cols(h)] * f_got[:, cols(h)]
        o = o + got_o[:, cols(h)].astype(F32) * f_far[:, cols(h)] + got_h[:, cols(h)].astype(F32) * f_h[:, cols(h)]
        out_ref[:, h * HD : (h + 1) * HD] = jnp.transpose(o).astype(BF16)

    for c in (q_to_sibling, q_to_partner, q_passed, o_copy, oml_copy) + hand_over(3, 0) + hand_over(1, 1):
        c.wait_send()
    own_across(gone)
    up(x, gone)

    @pl.when(z == 3)
    def _():
        q_help.wait_send()

    @pl.when(z == 0)
    def _():
        h_copy.wait_send()
        hml_copy.wait_send()
        for column in range(4):
            for c in share_copies(column) + (share_pass(column),):
                c.wait_send()

    relay(lambda mate: up(mate, gone), lambda plane: across(plane, gone))


def per_device(queries, key_rows, value_rows):
    return pl.pallas_call(
        kernel,
        out_shape=jax.ShapeDtypeStruct((ROWS, HEADS * HD), BF16),
        in_specs=[pl.BlockSpec(memory_space=pl.ANY)] * 3,
        out_specs=pl.BlockSpec(memory_space=pltpu.VMEM),
        scratch_shapes=[
            pltpu.VMEM((PLACES + 4 * EXTRA, 2 * ROWS, HD), BF16),
            pltpu.VMEM((ROWS, HD), BF16),
            pltpu.VMEM((SETS + 1, ROWS, HEADS * HD), BF16),
            pltpu.VMEM((SETS + 1, 2 * HD, COLS), BF16),
            pltpu.VMEM((SETS + 1, 16, COLS), F32),
            pltpu.VMEM((SETS + 1, HD, COLS), F32),
            pltpu.VMEM((KEYS, ROWS), F32),
            pltpu.VMEM((KEYS, ROWS), F32),
            pltpu.VMEM((KEYS, ROWS), BF16),
            pltpu.VMEM((KEYS, ROWS), BF16),
            pltpu.VMEM((8, ROWS), F32),
            pltpu.VMEM((8, ROWS), F32),
            pltpu.VMEM((2, HD, COLS), F32),
            pltpu.VMEM((2, 16, COLS), F32),
            pltpu.VMEM((HD, COLS), BF16),
            pltpu.VMEM((8, COLS), F32),
            pltpu.VMEM((HD, COLS), BF16),
            pltpu.VMEM((8, COLS), F32),
            pltpu.VMEM((HD, COLS), BF16),
            pltpu.VMEM((8, COLS), F32),
            pltpu.VMEM((HD, COLS), BF16),
            pltpu.VMEM((8, COLS), F32),
            pltpu.SemaphoreType.DMA((3,)),
            pltpu.SemaphoreType.DMA((4, 4)),
            pltpu.SemaphoreType.DMA((4, 4)),
            pltpu.SemaphoreType.DMA((PLACES + 4 * EXTRA,)),
            pltpu.SemaphoreType.DMA((3,)),
            pltpu.SemaphoreType.DMA((3,)),
            pltpu.SemaphoreType.DMA((2,)),
            pltpu.SemaphoreType.DMA((2,)),
            pltpu.SemaphoreType.DMA((2,)),
            pltpu.SemaphoreType.DMA((2,)),
            pltpu.SemaphoreType.DMA((2,)),
            pltpu.SemaphoreType.DMA((2,)),
            pltpu.SemaphoreType.DMA((3, 4)),
            pltpu.SemaphoreType.DMA((2,)),
            pltpu.SemaphoreType.DMA((2,)),
            pltpu.SemaphoreType.DMA((2,)),
        ],
        compiler_params=pltpu.CompilerParams(
            collective_id=0, has_side_effects=True, vmem_limit_bytes=60 << 20
        ),
        name="attend",
    )(queries, key_rows, value_rows)


def solution(mesh):
    placed = (P("ctx", "grp"), P("ctx", "grp"), P("ctx", "grp"))
    return jax.shard_map(
        per_device, mesh=mesh, in_specs=placed, out_specs=P("ctx", "grp"), check_vma=False
    )
```

```python
import math

import jax
import jax.numpy as jnp
from jax import lax
from jax.experimental import pallas as pl
from jax.experimental.pallas import tpu as pltpu
from jax.sharding import PartitionSpec as P

MESH = pl.DeviceIdType.MESH
F32 = jnp.float32
BF16 = jnp.bfloat16
LOW = -1e30
ROWS = 256
HD = 128
HEADS = 4
COLS = ROWS * HEADS
PLACES = 16
KEYS = 4 * ROWS
SETS = 4
HELP = 4
EXTRA = 3


def dot(a, b):
    return lax.dot_general(a, b, (((1,), (0,)), ((), ())), preferred_element_type=F32)


def kernel(
    q_in, k_in, v_in, out_ref,
    blocks, v_own, q_sets, q_t, ml_ref, acc, s_a, s_b, p_a, p_b, al_a, al_b,
    got_acc, got_ml, part_o, part_ml, got_o, got_oml, part_h, part_hml, got_h, got_hml,
    in_sem, x_sem, z_sem, from_sem, q_send, q_recv, acc_send, acc_recv, stat_send, stat_recv, o_sem, oml_sem,
    share_send, qh_sem, h_sem, hml_sem,
):
    ctx = lax.axis_index("ctx")
    grp = lax.axis_index("grp")
    place = ctx // 4
    y = (ctx // 2) % 2
    core = ctx % 2
    sibling = (ctx + 1 - 2 * core, grp)
    partner = (ctx + 2 - 4 * y, grp)
    z, x = place // 4, place % 4
    along_x = core == 0

    def at(other_place):
        return (other_place * 4 + y * 2 + core, grp)

    through = jnp.logical_or(jnp.logical_not(along_x), z < 3)
    helped = at(12 + x)
    helper = at(x)

    def mates(step):
        for dx in (1, 3, 2):
            mate = (x + dx) % 4
            step(mate, jnp.logical_or(through, mate > x), jnp.logical_or(through, mate < x))

    k_get = pltpu.make_async_copy(k_in, blocks.at[place, pl.ds(0, ROWS)], in_sem.at[0])
    v_get = pltpu.make_async_copy(v_in, v_own, in_sem.at[1])
    q_get = pltpu.make_async_copy(q_in, q_sets.at[0], in_sem.at[2])
    v_get.start()
    k_get.start()
    q_get.start()

    barrier = pltpu.get_barrier_semaphore()
    pl.semaphore_signal(barrier, inc=1, device_id=sibling, device_id_type=MESH)
    pl.semaphore_signal(barrier, inc=1, device_id=partner, device_id_type=MESH)

    def greet(mate, _, hears):
        @pl.when(hears)
        def _():
            pl.semaphore_signal(barrier, inc=1, device_id=at(z * 4 + mate), device_id_type=MESH)

    mates(greet)
    for below in range(3):
        @pl.when(below < z)
        def _(below=below):
            pl.semaphore_signal(barrier, inc=1, device_id=at(below * 4 + x), device_id_type=MESH)

    @pl.when(z == 0)
    def _():
        pl.semaphore_signal(barrier, inc=1, device_id=helped, device_id_type=MESH)

    ml_ref[:, :8] = jnp.full((SETS + 1, 8, COLS), LOW, F32)
    ml_ref[:, 8:] = jnp.zeros((SETS + 1, 8, COLS), F32)
    acc[...] = jnp.zeros(acc.shape, F32)

    @pl.when(z != 3)
    def _():
        got_h[...] = jnp.zeros(got_h.shape, BF16)
        got_hml[...] = jnp.full(got_hml.shape, LOW, F32)

    @pl.when(z == 0)
    def _():
        got_acc[1] = jnp.zeros((HD, COLS), F32)
        got_ml[1, :8] = jnp.full((8, COLS), LOW, F32)
        got_ml[1, 8:] = jnp.zeros((8, COLS), F32)
        got_o[...] = jnp.zeros(got_o.shape, BF16)
        got_oml[0:1] = jnp.full((1, COLS), LOW, F32)
        got_oml[1:] = jnp.zeros((7, COLS), F32)

    v_get.wait()
    v_t = jnp.transpose(v_own[...].astype(F32)).astype(BF16)
    blocks[place, ROWS : ROWS + HD] = v_t[:, :HD]
    blocks[place, ROWS + HD :] = v_t[:, HD:]
    k_get.wait()
    q_get.wait()

    pl.semaphore_wait(barrier, 5 - z + jnp.where(z == 3, 1, 0) + jnp.where(through, 3, 3 - x))

    def copy(src, dst, send, recv, device):
        return pltpu.make_async_remote_copy(
            src_ref=src, dst_ref=dst, send_sem=send, recv_sem=recv,
            device_id=device, device_id_type=MESH,
        )

    def along_x_copy(plane, mate):
        here = plane * 4 + x
        return copy(blocks.at[here], blocks.at[here], x_sem.at[plane, mate], from_sem.at[here], at(z * 4 + mate))

    def along_z_copy(column, above):
        here = z * 4 + column
        return copy(blocks.at[here], blocks.at[here], z_sem.at[column, above], from_sem.at[here], at(above * 4 + x))

    def wait_block(here):
        copy(blocks.at[here], blocks.at[here], x_sem.at[0, 0], from_sem.at[here], sibling).wait_recv()

    def up(column, step):
        for dz in (2, 1):
            @pl.when(z + dz < 4)
            def _(dz=dz):
                step(along_z_copy(column, z + dz))

    def across(plane, step):
        for dx in (1, 3, 2):
            step(along_x_copy(plane, (x + dx) % 4))

    def own_across(step):
        for dx in (1, 3, 2):
            mate = (x + dx) % 4

            @pl.when(jnp.logical_or(jnp.logical_or(jnp.logical_and(along_x, z < 3), z == 0), mate > x))
            def _(mate=mate):
                step(along_x_copy(z, mate))

    def share_copies(column):
        return (
            copy(blocks.at[column], blocks.at[16 + column], share_send.at[0, column], from_sem.at[16 + column], sibling),
            copy(blocks.at[column], blocks.at[20 + column], share_send.at[1, column], from_sem.at[20 + column], partner),
        )

    def share_pass(column):
        return copy(
            blocks.at[20 + column], blocks.at[24 + column], share_send.at[2, column], from_sem.at[24 + column], sibling
        )

    def share(column):
        @pl.when(z == 0)
        def _():
            for c in share_copies(column):
                c.start()

    def start(c):
        c.start()

    def gone(c):
        c.wait_send()

    q_to_sibling = copy(q_sets.at[0], q_sets.at[1], q_send.at[0], q_recv.at[0], sibling)
    q_to_partner = copy(q_sets.at[0], q_sets.at[2], q_send.at[1], q_recv.at[1], partner)
    q_help = copy(q_sets.at[0], q_sets.at[HELP], qh_sem.at[0], qh_sem.at[1], helper)
    h_copy = copy(part_h, got_h, h_sem.at[0], h_sem.at[1], helped)
    hml_copy = copy(part_hml, got_hml, hml_sem.at[0], hml_sem.at[1], helped)
    q_passed = copy(q_sets.at[2], q_sets.at[3], q_send.at[2], q_recv.at[2], sibling)

    @pl.when(z > 0)
    def _():
        q_to_sibling.start()

    @pl.when(core == 0)
    def _():
        own_across(start)

    @pl.when(core == 1)
    def _():
        up(x, start)

    @pl.when(z > 0)
    def _():
        q_to_partner.start()

    @pl.when(core == 0)
    def _():
        up(x, start)

    @pl.when(core == 1)
    def _():
        own_across(start)

    @pl.when(z == 3)
    def _():
        q_help.start()

    share(x)

    scale = math.log2(math.e) / math.sqrt(HD)

    def ready_queries(s):
        for h in range(HEADS):
            full = jnp.transpose(q_sets[s, :, h * HD : (h + 1) * HD].astype(F32)) * scale
            hi = full.astype(BF16)
            q_t[s, :HD, h * ROWS : (h + 1) * ROWS] = hi
            q_t[s, HD:, h * ROWS : (h + 1) * ROWS] = (full - hi.astype(F32)).astype(BF16)

    s_refs, p_refs, al_refs = (s_a, s_b), (p_a, p_b), (al_a, al_b)

    def keys(plane, count):
        k = jnp.concatenate([blocks[plane * 4 + i, :ROWS] for i in range(count)], 0)
        return jnp.concatenate([k, k], 1)

    def values(plane, count):
        tiles = []
        for i in range(count):
            tiles.append(blocks[plane * 4 + i, ROWS : ROWS + HD])
            tiles.append(blocks[plane * 4 + i, ROWS + HD :])
        return jnp.concatenate(tiles, 1)

    def cols(h):
        return slice(h * ROWS, (h + 1) * ROWS)

    def scores(s, k, h, slot):
        s_refs[slot][: k.shape[0]] = dot(k, q_t[s, :, cols(h)])

    def weigh(s, h, slot, n, visible):
        score = s_refs[slot][:n]
        if visible is not None:
            score = jnp.where(visible, score, LOW)
        old = ml_ref[s, :8, cols(h)]
        top = jnp.max(score.reshape(n // 8, 8, ROWS), axis=0)
        new = jnp.maximum(old, jnp.max(top, axis=0, keepdims=True))
        w = jnp.exp2(score - new[:1])
        if visible is not None:
            w = jnp.where(visible, w, 0.0)
        alpha = jnp.exp2(old - new)
        ml_ref[s, 8:, cols(h)] = ml_ref[s, 8:, cols(h)] * alpha + jnp.sum(w.reshape(n // 8, 8, ROWS), axis=0)
        p_refs[slot][:n] = w.astype(BF16)
        al_refs[slot][...] = alpha
        ml_ref[s, :8, cols(h)] = new

    def gather(s, v, h, slot):
        acc[s, :, cols(h)] = acc[s, :, cols(h)] * al_refs[slot][:1] + dot(v, p_refs[slot][: v.shape[1]])

    def tiles(list_of, visible=None):
        s, h, k, v = list_of[0]
        scores(s, k, h, 0)
        for n, (s, h, k, v) in enumerate(list_of):
            if n + 1 < len(list_of):
                s_next, h_next, k_next, _ = list_of[n + 1]
                scores(s_next, k_next, h_next, (n + 1) % 2)
            if n > 0:
                s_last, h_last, _, v_last = list_of[n - 1]
                gather(s_last, v_last, h_last, (n - 1) % 2)
            weigh(s, h, n % 2, k.shape[0], visible)
        s, h, k, v = list_of[-1]
        gather(s, v, h, (len(list_of) - 1) % 2)

    def own_block():
        key_at = lax.broadcasted_iota(jnp.int32, (ROWS, ROWS), 0)
        query_at = lax.broadcasted_iota(jnp.int32, (ROWS, ROWS), 1)
        k = blocks[place, :ROWS]
        k = jnp.concatenate([k, k], 1)
        v = jnp.concatenate([blocks[place, ROWS : ROWS + HD], blocks[place, ROWS + HD :]], 1)
        tiles([(0, h, k, v) for h in range(HEADS)], key_at <= query_at)

    def own_plane(s):
        set_at = jnp.where(s < 2, y, 1 - y) * 2 + jnp.where(s % 2 == 0, core, 1 - core)
        seen = x + jnp.where(set_at > y * 2 + core, 1, 0)
        first_places(s, z, seen)

    def first_places(s, plane, seen):
        for count in (1, 2, 3, 4):
            @pl.when(seen == count)
            def _(count=count):
                k, v = keys(plane, count), values(plane, count)
                tiles([(s, h, k, v) for h in range(HEADS)])

    def relay(step_up, step_across):
        @pl.when(core == 0)
        def _():
            for dx in (1, 3, 2):
                mate = (x + dx) % 4

                @pl.when(jnp.logical_or(through, mate < x))
                def _(mate=mate):
                    step_up(mate)

        @pl.when(core == 1)
        def _():
            for dz in (1, 2):
                @pl.when(z >= dz)
                def _(dz=dz):
                    step_across(z - dz)

    def relay_up(mate):
        wait_block(z * 4 + mate)
        up(mate, start)
        share(mate)

    def relay_across(plane):
        wait_block(plane * 4 + x)
        across(plane, start)

    def plane_at(t):
        return z - 1 - t

    def arrive(plane):
        for column in range(4):
            @pl.when(jnp.logical_or(along_x, x != column))
            def _(column=column):
                wait_block(plane * 4 + column)

    def hand_over(s, slot):
        return (
            copy(acc.at[s], got_acc.at[slot], acc_send.at[slot], acc_recv.at[slot], sibling),
            copy(ml_ref.at[s], got_ml.at[slot], stat_send.at[slot], stat_recv.at[slot], sibling),
        )

    def merged(s, slot):
        m, l = ml_ref[s, 0:1], jnp.sum(ml_ref[s, 8:], axis=0, keepdims=True)
        m_got, l_got = got_ml[slot, 0:1], jnp.sum(got_ml[slot, 8:], axis=0, keepdims=True)
        top = jnp.maximum(m, m_got)
        f, f_got = jnp.exp2(m - top), jnp.exp2(m_got - top)
        total = l * f + l_got * f_got
        return top, total, f, f_got

    ready_queries(0)
    own_block()

    @pl.when(z > 0)
    def _():
        q_to_sibling.wait_recv()
        ready_queries(1)

    relay(relay_up, relay_across)

    @pl.when(core == 1)
    def _():
        for column in range(4):
            @pl.when(jnp.logical_or(jnp.logical_and(z == 0, column != x), column < x))
            def _(column=column):
                wait_block(z * 4 + column)
                share(column)

    def plane_step(t, _):
        s = t + 1

        @pl.when(s == 2)
        def _():
            q_to_partner.wait_recv()
            q_passed.start()

        @pl.when(s == 3)
        def _():
            q_passed.wait_recv()

        @pl.when(s > 1)
        def _():
            ready_queries(s)

        own_plane(s)
        return 0

    lax.fori_loop(0, jnp.where(z > 0, 3, 0), plane_step, 0)

    def layers(s, lo, hi, plane_at=plane_at):
        @pl.when(lo < hi)
        def _():
            scores(s, keys(plane_at(lo), 4), 0, 0)
            p_b[...] = jnp.zeros(p_b.shape, BF16)
            al_b[...] = jnp.ones(al_b.shape, F32)

            def step(t, _):
                k, v = keys(plane_at(t), 4), values(plane_at(t), 4)
                k_next = keys(plane_at(jnp.minimum(t + 1, hi - 1)), 4)
                v_last = values(plane_at(jnp.maximum(t - 1, lo)), 4)
                for h in range(HEADS):
                    if h + 1 < HEADS:
                        scores(s, k, h + 1, (h + 1) % 2)
                    else:
                        scores(s, k_next, 0, 0)
                    if h > 0:
                        gather(s, v, h - 1, (h - 1) % 2)
                    else:
                        gather(s, v_last, HEADS - 1, 1)
                    weigh(s, h, h % 2, KEYS, None)
                return 0

            lax.fori_loop(lo, hi, step, 0)
            gather(s, values(plane_at(hi - 1), 4), HEADS - 1, 1)

    planes = jnp.minimum(z, 2)

    def siblings_partner(t, _):
        plane = plane_at(t)
        arrive(plane)
        k, v = keys(plane, 4), values(plane, 4)
        tiles([(3, h, k, v) for h in range(HEADS)])
        return 0

    lax.fori_loop(0, planes, siblings_partner, 0)

    @pl.when(z > 0)
    def _():
        for c in hand_over(3, 0):
            c.start()

    layers(2, 0, planes)

    def help_at(t):
        return jnp.where(t == 0, 0, t + 3)

    @pl.when(z == 0)
    def _():
        q_help.wait_recv()
        ready_queries(HELP)
        for column in range(4):
            wait_block(16 + column)
        layers(HELP, 0, 2, help_at)


    oml_copy = copy(part_ml, got_oml, oml_sem.at[0], oml_sem.at[1], partner)
    halves = [slice(half * COLS // 2, (half + 1) * COLS // 2) for half in range(2)]
    o_copies = [
        copy(part_o.at[:, part], got_o.at[:, part], o_sem.at[0, half], o_sem.at[1, half], partner)
        for half, part in enumerate(halves)
    ]

    @pl.when(z > 0)
    def _():
        for c in hand_over(3, 0):
            c.wait_recv()
        top, total, f, f_got = merged(2, 0)
        part_ml[0:1] = top
        part_ml[1:2] = total
        part_ml[2:] = jnp.zeros((6, COLS), F32)
        oml_copy.start()
        safe = 1.0 / jnp.where(total > 0, total, 1.0)
        f, f_got = f * safe, f_got * safe
        for part, c in zip(halves, o_copies):
            part_o[:, part] = (acc[2, :, part] * f[:, part] + got_acc[0, :, part] * f_got[:, part]).astype(BF16)
            c.start()

    layers(1, 0, planes)

    @pl.when(z > 0)
    def _():
        for c in hand_over(1, 1):
            c.start()

    own_plane(0)
    layers(0, 0, planes)

    @pl.when(z == 0)
    def _():
        for column in range(4):
            wait_block(20 + column)
            share_pass(column).start()
        layers(HELP, 2, 3, help_at)
        for column in range(4):
            wait_block(24 + column)
        layers(HELP, 3, 4, help_at)
        l_h = jnp.sum(ml_ref[HELP, 8:], axis=0, keepdims=True)
        part_hml[0:1] = ml_ref[HELP, 0:1]
        part_hml[1:2] = l_h
        part_hml[2:] = jnp.zeros((6, COLS), F32)
        part_h[...] = (acc[HELP] * (1.0 / l_h)).astype(BF16)
        h_copy.start()
        hml_copy.start()

        def other_blocks(e, _):
            first_places(0, 4 + e, x + jnp.where(e == 0, core, y))
            return 0

        lax.fori_loop(0, EXTRA, other_blocks, 0)

    @pl.when(z > 0)
    def _():
        for c in hand_over(1, 1):
            c.wait_recv()
        oml_copy.wait_recv()

    m_own, total, f, f_got = merged(0, 1)

    @pl.when(z == 3)
    def _():
        h_copy.wait_recv()
        hml_copy.wait_recv()

    m_got, m_h = got_oml[0:1], got_hml[0:1]
    top = jnp.maximum(jnp.maximum(m_own, m_got), m_h)
    a_own = jnp.exp2(m_own - top)
    a_got = jnp.exp2(m_got - top) * got_oml[1:2]
    a_h = jnp.where(z == 3, jnp.exp2(m_h - top) * got_hml[1:2], 0.0)
    inv = 1.0 / (total * a_own + a_got + a_h)
    f, f_got, f_far, f_h = f * (a_own * inv), f_got * (a_own * inv), a_got * inv, a_h * inv
    for h in range(HEADS):
        if h % 2 == 0:
            @pl.when(z > 0)
            def _(h=h):
                o_copies[h // 2].wait_recv()

        o = acc[0, :, cols(h)] * f[:, cols(h)] + got_acc[1, :, cols(h)] * f_got[:, cols(h)]
        o = o + got_o[:, cols(h)].astype(F32) * f_far[:, cols(h)] + got_h[:, cols(h)].astype(F32) * f_h[:, cols(h)]
        out_ref[:, h * HD : (h + 1) * HD] = jnp.transpose(o).astype(BF16)

    @pl.when(z > 0)
    def _():
        for c in (q_to_sibling, q_to_partner, q_passed, oml_copy, *o_copies) + hand_over(3, 0) + hand_over(1, 1):
            c.wait_send()

    own_across(gone)
    up(x, gone)

    @pl.when(z == 3)
    def _():
        q_help.wait_send()

    @pl.when(z == 0)
    def _():
        h_copy.wait_send()
        hml_copy.wait_send()
        for column in range(4):
            for c in share_copies(column) + (share_pass(column),):
                c.wait_send()

    relay(lambda mate: up(mate, gone), lambda plane: across(plane, gone))


def per_device(queries, key_rows, value_rows):
    return pl.pallas_call(
        kernel,
        out_shape=jax.ShapeDtypeStruct((ROWS, HEADS * HD), BF16),
        in_specs=[pl.BlockSpec(memory_space=pl.ANY)] * 3,
        out_specs=pl.BlockSpec(memory_space=pltpu.VMEM),
        scratch_shapes=[
            pltpu.VMEM((PLACES + 4 * EXTRA, 2 * ROWS, HD), BF16),
            pltpu.VMEM((ROWS, HD), BF16),
            pltpu.VMEM((SETS + 1, ROWS, HEADS * HD), BF16),
            pltpu.VMEM((SETS + 1, 2 * HD, COLS), BF16),
            pltpu.VMEM((SETS + 1, 16, COLS), F32),
            pltpu.VMEM((SETS + 1, HD, COLS), F32),
            pltpu.VMEM((KEYS, ROWS), F32),
            pltpu.VMEM((KEYS, ROWS), F32),
            pltpu.VMEM((KEYS, ROWS), BF16),
            pltpu.VMEM((KEYS, ROWS), BF16),
            pltpu.VMEM((8, ROWS), F32),
            pltpu.VMEM((8, ROWS), F32),
            pltpu.VMEM((2, HD, COLS), F32),
            pltpu.VMEM((2, 16, COLS), F32),
            pltpu.VMEM((HD, COLS), BF16),
            pltpu.VMEM((8, COLS), F32),
            pltpu.VMEM((HD, COLS), BF16),
            pltpu.VMEM((8, COLS), F32),
            pltpu.VMEM((HD, COLS), BF16),
            pltpu.VMEM((8, COLS), F32),
            pltpu.VMEM((HD, COLS), BF16),
            pltpu.VMEM((8, COLS), F32),
            pltpu.SemaphoreType.DMA((3,)),
            pltpu.SemaphoreType.DMA((4, 4)),
            pltpu.SemaphoreType.DMA((4, 4)),
            pltpu.SemaphoreType.DMA((PLACES + 4 * EXTRA,)),
            pltpu.SemaphoreType.DMA((3,)),
            pltpu.SemaphoreType.DMA((3,)),
            pltpu.SemaphoreType.DMA((2,)),
            pltpu.SemaphoreType.DMA((2,)),
            pltpu.SemaphoreType.DMA((2,)),
            pltpu.SemaphoreType.DMA((2,)),
            pltpu.SemaphoreType.DMA((2, 2)),
            pltpu.SemaphoreType.DMA((2,)),
            pltpu.SemaphoreType.DMA((3, 4)),
            pltpu.SemaphoreType.DMA((2,)),
            pltpu.SemaphoreType.DMA((2,)),
            pltpu.SemaphoreType.DMA((2,)),
        ],
        compiler_params=pltpu.CompilerParams(
            collective_id=0, has_side_effects=True, vmem_limit_bytes=60 << 20
        ),
        name="attend",
    )(queries, key_rows, value_rows)


def solution(mesh):
    placed = (P("ctx", "grp"), P("ctx", "grp"), P("ctx", "grp"))
    return jax.shard_map(
        per_device, mesh=mesh, in_specs=placed, out_specs=P("ctx", "grp"), check_vma=False
    )
```

```python
import math

import jax
import jax.numpy as jnp
from jax import lax
from jax.experimental import pallas as pl
from jax.experimental.pallas import tpu as pltpu
from jax.sharding import PartitionSpec as P

MESH = pl.DeviceIdType.MESH
F32 = jnp.float32
BF16 = jnp.bfloat16
LOW = -1e30
ROWS = 256
HD = 128
HEADS = 4
COLS = ROWS * HEADS
PLACES = 16
KEYS = 4 * ROWS
SETS = 4
HELP = 4
EXTRA = 3


def dot(a, b):
    return lax.dot_general(a, b, (((1,), (0,)), ((), ())), preferred_element_type=F32)


def kernel(
    q_in, k_in, v_in, out_ref,
    blocks, v_own, q_sets, q_t, ml_ref, acc, s_a, s_b, p_a, p_b, al_a, al_b,
    got_acc, got_ml, part_o, part_ml, got_o, got_oml, part_h, part_hml, got_h, got_hml,
    in_sem, x_sem, z_sem, from_sem, q_send, q_recv, acc_send, acc_recv, stat_send, stat_recv, o_sem, oml_sem,
    share_send, qh_sem, h_sem, hml_sem, out_buf, out_sem,
):
    ctx = lax.axis_index("ctx")
    grp = lax.axis_index("grp")
    place = ctx // 4
    y = (ctx // 2) % 2
    core = ctx % 2
    sibling = (ctx + 1 - 2 * core, grp)
    partner = (ctx + 2 - 4 * y, grp)
    z, x = place // 4, place % 4
    along_x = core == 0

    def at(other_place):
        return (other_place * 4 + y * 2 + core, grp)

    through = jnp.logical_or(jnp.logical_not(along_x), z < 3)
    helped = at(12 + x)
    helper = at(x)

    def mates(step):
        for dx in (1, 3, 2):
            mate = (x + dx) % 4
            step(mate, jnp.logical_or(through, mate > x), jnp.logical_or(through, mate < x))

    k_get = pltpu.make_async_copy(k_in, blocks.at[place, pl.ds(0, ROWS)], in_sem.at[0])
    v_get = pltpu.make_async_copy(v_in, v_own, in_sem.at[1])
    q_get = pltpu.make_async_copy(q_in, q_sets.at[0], in_sem.at[2])
    v_get.start()
    k_get.start()
    q_get.start()

    barrier = pltpu.get_barrier_semaphore()
    pl.semaphore_signal(barrier, inc=1, device_id=sibling, device_id_type=MESH)
    pl.semaphore_signal(barrier, inc=1, device_id=partner, device_id_type=MESH)

    def greet(mate, _, hears):
        @pl.when(hears)
        def _():
            pl.semaphore_signal(barrier, inc=1, device_id=at(z * 4 + mate), device_id_type=MESH)

    mates(greet)
    for below in range(3):
        @pl.when(below < z)
        def _(below=below):
            pl.semaphore_signal(barrier, inc=1, device_id=at(below * 4 + x), device_id_type=MESH)

    @pl.when(z == 0)
    def _():
        pl.semaphore_signal(barrier, inc=1, device_id=helped, device_id_type=MESH)

    ml_ref[:, :8] = jnp.full((SETS + 1, 8, COLS), LOW, F32)
    ml_ref[:, 8:] = jnp.zeros((SETS + 1, 8, COLS), F32)
    acc[...] = jnp.zeros(acc.shape, F32)

    @pl.when(z != 3)
    def _():
        got_h[...] = jnp.zeros(got_h.shape, BF16)
        got_hml[...] = jnp.full(got_hml.shape, LOW, F32)

    @pl.when(z == 0)
    def _():
        got_acc[1] = jnp.zeros((HD, COLS), F32)
        got_ml[1, :8] = jnp.full((8, COLS), LOW, F32)
        got_ml[1, 8:] = jnp.zeros((8, COLS), F32)
        got_o[...] = jnp.zeros(got_o.shape, BF16)
        got_oml[0:1] = jnp.full((1, COLS), LOW, F32)
        got_oml[1:] = jnp.zeros((7, COLS), F32)

    v_get.wait()
    v_t = jnp.transpose(v_own[...].astype(F32)).astype(BF16)
    blocks[place, ROWS : ROWS + HD] = v_t[:, :HD]
    blocks[place, ROWS + HD :] = v_t[:, HD:]
    k_get.wait()
    q_get.wait()

    pl.semaphore_wait(barrier, 5 - z + jnp.where(z == 3, 1, 0) + jnp.where(through, 3, 3 - x))

    def copy(src, dst, send, recv, device):
        return pltpu.make_async_remote_copy(
            src_ref=src, dst_ref=dst, send_sem=send, recv_sem=recv,
            device_id=device, device_id_type=MESH,
        )

    def along_x_copy(plane, mate):
        here = plane * 4 + x
        return copy(blocks.at[here], blocks.at[here], x_sem.at[plane, mate], from_sem.at[here], at(z * 4 + mate))

    def along_z_copy(column, above):
        here = z * 4 + column
        return copy(blocks.at[here], blocks.at[here], z_sem.at[column, above], from_sem.at[here], at(above * 4 + x))

    def wait_block(here):
        copy(blocks.at[here], blocks.at[here], x_sem.at[0, 0], from_sem.at[here], sibling).wait_recv()

    def up(column, step):
        for dz in (2, 1):
            @pl.when(z + dz < 4)
            def _(dz=dz):
                step(along_z_copy(column, z + dz))

    def across(plane, step):
        for dx in (1, 3, 2):
            step(along_x_copy(plane, (x + dx) % 4))

    def own_across(step):
        for dx in (1, 3, 2):
            mate = (x + dx) % 4

            @pl.when(jnp.logical_or(jnp.logical_or(jnp.logical_and(along_x, z < 3), z == 0), mate > x))
            def _(mate=mate):
                step(along_x_copy(z, mate))

    def share_copies(column):
        return (
            copy(blocks.at[column], blocks.at[16 + column], share_send.at[0, column], from_sem.at[16 + column], sibling),
            copy(blocks.at[column], blocks.at[20 + column], share_send.at[1, column], from_sem.at[20 + column], partner),
        )

    def share_pass(column):
        return copy(
            blocks.at[20 + column], blocks.at[24 + column], share_send.at[2, column], from_sem.at[24 + column], sibling
        )

    def share(column):
        @pl.when(z == 0)
        def _():
            for c in share_copies(column):
                c.start()

    def put(h):
        part = pl.ds(h * HD, HD)
        return pltpu.make_async_copy(out_buf.at[:, part], out_ref.at[:, part], out_sem.at[h])

    def start(c):
        c.start()

    def gone(c):
        c.wait_send()

    q_to_sibling = copy(q_sets.at[0], q_sets.at[1], q_send.at[0], q_recv.at[0], sibling)
    q_to_partner = copy(q_sets.at[0], q_sets.at[2], q_send.at[1], q_recv.at[1], partner)
    q_help = copy(q_sets.at[0], q_sets.at[HELP], qh_sem.at[0], qh_sem.at[1], helper)
    h_copy = copy(part_h, got_h, h_sem.at[0], h_sem.at[1], helped)
    hml_copy = copy(part_hml, got_hml, hml_sem.at[0], hml_sem.at[1], helped)
    q_passed = copy(q_sets.at[2], q_sets.at[3], q_send.at[2], q_recv.at[2], sibling)

    @pl.when(z > 0)
    def _():
        q_to_partner.start()
        q_to_sibling.start()

    @pl.when(core == 0)
    def _():
        own_across(start)

    @pl.when(core == 1)
    def _():
        up(x, start)

    @pl.when(core == 0)
    def _():
        up(x, start)

    @pl.when(core == 1)
    def _():
        own_across(start)

    @pl.when(z == 3)
    def _():
        q_help.start()

    share(x)

    scale = math.log2(math.e) / math.sqrt(HD)

    def ready_queries(s):
        for h in range(HEADS):
            full = jnp.transpose(q_sets[s, :, h * HD : (h + 1) * HD].astype(F32)) * scale
            hi = full.astype(BF16)
            q_t[s, :HD, h * ROWS : (h + 1) * ROWS] = hi
            q_t[s, HD:, h * ROWS : (h + 1) * ROWS] = (full - hi.astype(F32)).astype(BF16)

    s_refs, p_refs, al_refs = (s_a, s_b), (p_a, p_b), (al_a, al_b)

    def keys(plane, count):
        k = jnp.concatenate([blocks[plane * 4 + i, :ROWS] for i in range(count)], 0)
        return jnp.concatenate([k, k], 1)

    def values(plane, count):
        tiles = []
        for i in range(count):
            tiles.append(blocks[plane * 4 + i, ROWS : ROWS + HD])
            tiles.append(blocks[plane * 4 + i, ROWS + HD :])
        return jnp.concatenate(tiles, 1)

    def cols(h):
        return slice(h * ROWS, (h + 1) * ROWS)

    def scores(s, k, h, slot):
        s_refs[slot][: k.shape[0]] = dot(k, q_t[s, :, cols(h)])

    def weigh(s, h, slot, n, visible):
        score = s_refs[slot][:n]
        if visible is not None:
            score = jnp.where(visible, score, LOW)
        old = ml_ref[s, :8, cols(h)]
        top = jnp.max(score.reshape(n // 8, 8, ROWS), axis=0)
        new = jnp.maximum(old, jnp.max(top, axis=0, keepdims=True))
        w = jnp.exp2(score - new[:1])
        if visible is not None:
            w = jnp.where(visible, w, 0.0)
        alpha = jnp.exp2(old - new)
        ml_ref[s, 8:, cols(h)] = ml_ref[s, 8:, cols(h)] * alpha + jnp.sum(w.reshape(n // 8, 8, ROWS), axis=0)
        p_refs[slot][:n] = w.astype(BF16)
        al_refs[slot][...] = alpha
        ml_ref[s, :8, cols(h)] = new

    def gather(s, v, h, slot):
        acc[s, :, cols(h)] = acc[s, :, cols(h)] * al_refs[slot][:1] + dot(v, p_refs[slot][: v.shape[1]])

    def tiles(list_of, visible=None):
        s, h, k, v = list_of[0]
        scores(s, k, h, 0)
        for n, (s, h, k, v) in enumerate(list_of):
            if n + 1 < len(list_of):
                s_next, h_next, k_next, _ = list_of[n + 1]
                scores(s_next, k_next, h_next, (n + 1) % 2)
            if n > 0:
                s_last, h_last, _, v_last = list_of[n - 1]
                gather(s_last, v_last, h_last, (n - 1) % 2)
            weigh(s, h, n % 2, k.shape[0], visible)
        s, h, k, v = list_of[-1]
        gather(s, v, h, (len(list_of) - 1) % 2)

    def own_block():
        key_at = lax.broadcasted_iota(jnp.int32, (ROWS, ROWS), 0)
        query_at = lax.broadcasted_iota(jnp.int32, (ROWS, ROWS), 1)
        k = blocks[place, :ROWS]
        k = jnp.concatenate([k, k], 1)
        v = jnp.concatenate([blocks[place, ROWS : ROWS + HD], blocks[place, ROWS + HD :]], 1)
        tiles([(0, h, k, v) for h in range(HEADS)], key_at <= query_at)

    def own_plane(s):
        set_at = jnp.where(s < 2, y, 1 - y) * 2 + jnp.where(s % 2 == 0, core, 1 - core)
        seen = x + jnp.where(set_at > y * 2 + core, 1, 0)
        first_places(s, z, seen)

    def first_places(s, plane, seen):
        for count in (1, 2, 3, 4):
            @pl.when(seen == count)
            def _(count=count):
                k, v = keys(plane, count), values(plane, count)
                tiles([(s, h, k, v) for h in range(HEADS)])

    def relay(step_up, step_across):
        @pl.when(core == 0)
        def _():
            for dx in (1, 3, 2):
                mate = (x + dx) % 4

                @pl.when(jnp.logical_or(through, mate < x))
                def _(mate=mate):
                    step_up(mate)

        @pl.when(core == 1)
        def _():
            for dz in (1, 2):
                @pl.when(z >= dz)
                def _(dz=dz):
                    step_across(z - dz)

    def relay_up(mate):
        wait_block(z * 4 + mate)
        up(mate, start)
        share(mate)

    def relay_across(plane):
        wait_block(plane * 4 + x)
        across(plane, start)

    def plane_at(t):
        return z - 1 - t

    def arrive(plane):
        for column in range(4):
            @pl.when(jnp.logical_or(along_x, x != column))
            def _(column=column):
                wait_block(plane * 4 + column)

    def hand_over(s, slot):
        return (
            copy(acc.at[s], got_acc.at[slot], acc_send.at[slot], acc_recv.at[slot], sibling),
            copy(ml_ref.at[s], got_ml.at[slot], stat_send.at[slot], stat_recv.at[slot], sibling),
        )

    def merged(s, slot):
        m, l = ml_ref[s, 0:1], jnp.sum(ml_ref[s, 8:], axis=0, keepdims=True)
        m_got, l_got = got_ml[slot, 0:1], jnp.sum(got_ml[slot, 8:], axis=0, keepdims=True)
        top = jnp.maximum(m, m_got)
        f, f_got = jnp.exp2(m - top), jnp.exp2(m_got - top)
        total = l * f + l_got * f_got
        return top, total, f, f_got

    ready_queries(0)
    own_block()

    @pl.when(z > 0)
    def _():
        q_to_sibling.wait_recv()
        ready_queries(1)

    relay(relay_up, relay_across)

    @pl.when(core == 1)
    def _():
        for column in range(4):
            @pl.when(jnp.logical_or(jnp.logical_and(z == 0, column != x), column < x))
            def _(column=column):
                wait_block(z * 4 + column)
                share(column)

    def plane_step(t, _):
        s = t + 1

        @pl.when(s == 2)
        def _():
            q_to_partner.wait_recv()
            q_passed.start()

        @pl.when(s == 3)
        def _():
            q_passed.wait_recv()

        @pl.when(s > 1)
        def _():
            ready_queries(s)

        own_plane(s)
        return 0

    lax.fori_loop(0, jnp.where(z > 0, 3, 0), plane_step, 0)

    def layers(s, lo, hi, plane_at=plane_at):
        @pl.when(lo < hi)
        def _():
            scores(s, keys(plane_at(lo), 4), 0, 0)
            p_b[...] = jnp.zeros(p_b.shape, BF16)
            al_b[...] = jnp.ones(al_b.shape, F32)

            def step(t, _):
                k, v = keys(plane_at(t), 4), values(plane_at(t), 4)
                k_next = keys(plane_at(jnp.minimum(t + 1, hi - 1)), 4)
                v_last = values(plane_at(jnp.maximum(t - 1, lo)), 4)
                for h in range(HEADS):
                    if h + 1 < HEADS:
                        scores(s, k, h + 1, (h + 1) % 2)
                    else:
                        scores(s, k_next, 0, 0)
                    if h > 0:
                        gather(s, v, h - 1, (h - 1) % 2)
                    else:
                        gather(s, v_last, HEADS - 1, 1)
                    weigh(s, h, h % 2, KEYS, None)
                return 0

            lax.fori_loop(lo, hi, step, 0)
            gather(s, values(plane_at(hi - 1), 4), HEADS - 1, 1)

    planes = jnp.minimum(z, 2)

    def siblings_partner(t, _):
        plane = plane_at(t)
        arrive(plane)
        k, v = keys(plane, 4), values(plane, 4)
        tiles([(3, h, k, v) for h in range(HEADS)])
        return 0

    lax.fori_loop(0, planes, siblings_partner, 0)

    @pl.when(z > 0)
    def _():
        for c in hand_over(3, 0):
            c.start()

    layers(2, 0, planes)

    def help_at(t):
        return jnp.where(t == 0, 0, t + 3)

    @pl.when(z == 0)
    def _():
        q_help.wait_recv()
        ready_queries(HELP)
        for column in range(4):
            wait_block(16 + column)
        layers(HELP, 0, 2, help_at)


    oml_copy = copy(part_ml, got_oml, oml_sem.at[0], oml_sem.at[1], partner)
    halves = [slice(half * COLS // 2, (half + 1) * COLS // 2) for half in range(2)]
    o_copies = [
        copy(part_o.at[:, part], got_o.at[:, part], o_sem.at[0, half], o_sem.at[1, half], partner)
        for half, part in enumerate(halves)
    ]

    @pl.when(z > 0)
    def _():
        for c in hand_over(3, 0):
            c.wait_recv()
        top, total, f, f_got = merged(2, 0)
        part_ml[0:1] = top
        part_ml[1:2] = total
        part_ml[2:] = jnp.zeros((6, COLS), F32)
        oml_copy.start()
        safe = 1.0 / jnp.where(total > 0, total, 1.0)
        f, f_got = f * safe, f_got * safe
        for part, c in zip(halves, o_copies):
            part_o[:, part] = (acc[2, :, part] * f[:, part] + got_acc[0, :, part] * f_got[:, part]).astype(BF16)
            c.start()

    layers(1, 0, planes)

    @pl.when(z > 0)
    def _():
        for c in hand_over(1, 1):
            c.start()

    own_plane(0)
    layers(0, 0, planes)

    @pl.when(z == 0)
    def _():
        for column in range(4):
            wait_block(20 + column)
            share_pass(column).start()
        layers(HELP, 2, 3, help_at)
        for column in range(4):
            wait_block(24 + column)
        layers(HELP, 3, 4, help_at)
        l_h = jnp.sum(ml_ref[HELP, 8:], axis=0, keepdims=True)
        part_hml[0:1] = ml_ref[HELP, 0:1]
        part_hml[1:2] = l_h
        part_hml[2:] = jnp.zeros((6, COLS), F32)
        part_h[...] = (acc[HELP] * (1.0 / l_h)).astype(BF16)
        h_copy.start()
        hml_copy.start()

        def other_blocks(e, _):
            first_places(0, 4 + e, x + jnp.where(e == 0, core, y))
            return 0

        lax.fori_loop(0, EXTRA, other_blocks, 0)

    @pl.when(z > 0)
    def _():
        for c in hand_over(1, 1):
            c.wait_recv()
        oml_copy.wait_recv()

    m_own, total, f, f_got = merged(0, 1)

    @pl.when(z == 3)
    def _():
        h_copy.wait_recv()
        hml_copy.wait_recv()

    m_got, m_h = got_oml[0:1], got_hml[0:1]
    top = jnp.maximum(jnp.maximum(m_own, m_got), m_h)
    a_own = jnp.exp2(m_own - top)
    a_got = jnp.exp2(m_got - top) * got_oml[1:2]
    a_h = jnp.where(z == 3, jnp.exp2(m_h - top) * got_hml[1:2], 0.0)
    inv = 1.0 / (total * a_own + a_got + a_h)
    f, f_got, f_far, f_h = f * (a_own * inv), f_got * (a_own * inv), a_got * inv, a_h * inv
    for h in range(HEADS):
        if h % 2 == 0:
            @pl.when(z > 0)
            def _(h=h):
                o_copies[h // 2].wait_recv()

        o = acc[0, :, cols(h)] * f[:, cols(h)] + got_acc[1, :, cols(h)] * f_got[:, cols(h)]
        o = o + got_o[:, cols(h)].astype(F32) * f_far[:, cols(h)] + got_h[:, cols(h)].astype(F32) * f_h[:, cols(h)]
        out_buf[:, h * HD : (h + 1) * HD] = jnp.transpose(o).astype(BF16)
        put(h).start()

    for h in range(HEADS):
        put(h).wait()

    @pl.when(z > 0)
    def _():
        for c in (q_to_sibling, q_to_partner, q_passed, oml_copy, *o_copies) + hand_over(3, 0) + hand_over(1, 1):
            c.wait_send()

    own_across(gone)
    up(x, gone)

    @pl.when(z == 3)
    def _():
        q_help.wait_send()

    @pl.when(z == 0)
    def _():
        h_copy.wait_send()
        hml_copy.wait_send()
        for column in range(4):
            for c in share_copies(column) + (share_pass(column),):
                c.wait_send()

    relay(lambda mate: up(mate, gone), lambda plane: across(plane, gone))


def per_device(queries, key_rows, value_rows):
    return pl.pallas_call(
        kernel,
        out_shape=jax.ShapeDtypeStruct((ROWS, HEADS * HD), BF16),
        in_specs=[pl.BlockSpec(memory_space=pl.ANY)] * 3,
        out_specs=pl.BlockSpec(memory_space=pl.ANY),
        scratch_shapes=[
            pltpu.VMEM((PLACES + 4 * EXTRA, 2 * ROWS, HD), BF16),
            pltpu.VMEM((ROWS, HD), BF16),
            pltpu.VMEM((SETS + 1, ROWS, HEADS * HD), BF16),
            pltpu.VMEM((SETS + 1, 2 * HD, COLS), BF16),
            pltpu.VMEM((SETS + 1, 16, COLS), F32),
            pltpu.VMEM((SETS + 1, HD, COLS), F32),
            pltpu.VMEM((KEYS, ROWS), F32),
            pltpu.VMEM((KEYS, ROWS), F32),
            pltpu.VMEM((KEYS, ROWS), BF16),
            pltpu.VMEM((KEYS, ROWS), BF16),
            pltpu.VMEM((8, ROWS), F32),
            pltpu.VMEM((8, ROWS), F32),
            pltpu.VMEM((2, HD, COLS), F32),
            pltpu.VMEM((2, 16, COLS), F32),
            pltpu.VMEM((HD, COLS), BF16),
            pltpu.VMEM((8, COLS), F32),
            pltpu.VMEM((HD, COLS), BF16),
            pltpu.VMEM((8, COLS), F32),
            pltpu.VMEM((HD, COLS), BF16),
            pltpu.VMEM((8, COLS), F32),
            pltpu.VMEM((HD, COLS), BF16),
            pltpu.VMEM((8, COLS), F32),
            pltpu.SemaphoreType.DMA((3,)),
            pltpu.SemaphoreType.DMA((4, 4)),
            pltpu.SemaphoreType.DMA((4, 4)),
            pltpu.SemaphoreType.DMA((PLACES + 4 * EXTRA,)),
            pltpu.SemaphoreType.DMA((3,)),
            pltpu.SemaphoreType.DMA((3,)),
            pltpu.SemaphoreType.DMA((2,)),
            pltpu.SemaphoreType.DMA((2,)),
            pltpu.SemaphoreType.DMA((2,)),
            pltpu.SemaphoreType.DMA((2,)),
            pltpu.SemaphoreType.DMA((2, 2)),
            pltpu.SemaphoreType.DMA((2,)),
            pltpu.SemaphoreType.DMA((3, 4)),
            pltpu.SemaphoreType.DMA((2,)),
            pltpu.SemaphoreType.DMA((2,)),
            pltpu.SemaphoreType.DMA((2,)),
            pltpu.VMEM((ROWS, HEADS * HD), BF16),
            pltpu.SemaphoreType.DMA((HEADS,)),
        ],
        compiler_params=pltpu.CompilerParams(
            collective_id=0, has_side_effects=True, vmem_limit_bytes=60 << 20
        ),
        name="attend",
    )(queries, key_rows, value_rows)


def solution(mesh):
    placed = (P("ctx", "grp"), P("ctx", "grp"), P("ctx", "grp"))
    return jax.shard_map(
        per_device, mesh=mesh, in_specs=placed, out_specs=P("ctx", "grp"), check_vma=False
    )
```
